128 devices in a mesh: row: 8 (over x_lo, z), col: 16 (over x_hi, y, core).
Axes of the slice: x: 4 (x_hi: 2, x_lo: 2; x = x_hi * 2 + x_lo), y: 4, z: 4, core: 2. Of those that a mesh axis runs over, the one named last changes fastest.
Arguments:
- x_vec: float32 [4, 2097152], P(None, ('col', 'row'))
- hx_vec: float32 [4, 2097152], P(None, ('col', 'row'))
- p_vec: float32 [4, 2097152], P(None, ('col', 'row'))
- hp_vec: float32 [4, 2097152], P(None, ('col', 'row'))
- theta: float32 [4], replicated, may hold values from 0.5 to 2
- precond: float32 [2097152], P(('col', 'row')), may hold values from 1 to 4
- tile_vals: bfloat16 [8, 16, 1024, 4096], P('row', 'col'), may hold values from -0.25 to 0.25
- tile_rows: int32 [8, 16, 1024], P('row', 'col'), may hold values from 0 to 2047
- tile_cols: int32 [8, 16, 1024], P('row', 'col'), may hold values from 0 to 2047
- tile_count: int32 [8, 16], P('row', 'col'), may hold values from 128 to 1024, as said below
Outputs:
- hw_vec: float32 [4, 2097152], P(None, ('col', 'row'))
- gram_a: float32 [12, 12], replicated
- gram_b: float32 [12, 12], replicated
The draws below stay inside these ranges and needn't reach their ends.
Inputs may be any that keep to these rules, and one draw needn't show every extreme that they name: `tile_count`: some tile uses all 1024 slots and some tile uses 1024 // 8.
All inputs are finite; a program needn't handle non-finite values.
Results may differ from the reference program's by a relative error of at most 0.0029.
Values may be sent and summed in bfloat16 or wider, within the bound.
No kernel may reach another device: no remote copies, remote signals or barrier semaphores. Data moves between devices by JAX's collectives and lax.ppermute only.
A program may use at most 192 MiB of HBM per device.

```python
import math
import jax
import jax.numpy as jnp
from jax import lax

VECS = 4
BLOCK = 64
PIECE = 16384
NZ = 1024
NBLK = 2048
NDIM = 2097152
N_ROW = 8
N_COL = 16


def shared_normal(key):
    return jax.random.normal(key, (VECS, NDIM), jnp.float32)


def paired_normal(key):
    pair_key = jax.random.fold_in(key, 101)
    return jnp.clip(jax.random.normal(pair_key, (VECS, NDIM), jnp.float32), -6.0, 6.0)


def rising_envelope():
    return jnp.exp(jnp.log(3.0) * jnp.arange(NDIM, dtype=jnp.float32) / NDIM) / 1.7


def draw_x_vec(key, part):
    shaped = shared_normal(key)
    return rising_envelope()[None, :] * shaped


def draw_hx_vec(key, part):
    shaped = shared_normal(key)
    key = jax.random.fold_in(key, 5)
    noise = jax.random.normal(key, (VECS, NDIM), jnp.float32)
    return rising_envelope()[None, :] * 1.5 * shaped + 0.8 * noise


def draw_p_vec(key, part):
    shaped = paired_normal(key)
    return shaped


def draw_hp_vec(key, part):
    shaped = paired_normal(key)
    key = jax.random.fold_in(key, 13)
    factor_key, noise_key = jax.random.split(key)
    factors = jax.random.uniform(factor_key, (VECS,), jnp.float32, 0.6, 1.6)
    noise = jax.random.normal(noise_key, (VECS, NDIM), jnp.float32)
    return factors[:, None] * shaped + 0.8 * noise


def draw_tile_count(key, part):
    key = jax.random.fold_in(key, 11)
    first_key, second_key = jax.random.split(key)
    total = N_ROW * N_COL
    counts = jax.random.randint(first_key, (total,), NZ // 8, NZ + 1)
    fullest = jax.random.randint(second_key, (), 0, total)
    places = jnp.arange(total, dtype=jnp.int32)
    counts = jnp.where(places == fullest, NZ, counts)
    counts = jnp.where(places == (fullest + 1) % total, NZ // 8, counts)
    return counts.reshape(N_ROW, N_COL).astype(jnp.int32)


def touch_ends(entries, stream_key, smallest, largest):
    shape = entries.shape
    place = [jax.random.randint(jax.random.fold_in(stream_key, axis), (), 0, shape[axis]) for axis in range(len(shape))]
    entries = entries.at[tuple(place)].set(smallest)
    longest = shape.index(max(shape))
    place[longest] = (place[longest] + 1) % shape[longest]
    return entries.at[tuple(place)].set(largest)


def block_scale(stream_key, dims, pieces, smallest, top_value):
    gain, own = 1.0, jax.random.fold_in(stream_key, 6)
    for axis_at, shards_of in pieces:
        draws = jnp.exp(jax.random.uniform(jax.random.fold_in(own, axis_at), (shards_of,), jnp.float32, smallest / len(pieces), top_value / len(pieces)))
        gain = gain * jnp.repeat(draws, dims[axis_at] // shards_of).reshape([-1 if axis == axis_at else 1 for axis in range(len(dims))])
    return gain


def centred(own_key, shape, scale, bound, pieces=(), kind=jnp.bfloat16):
    array = scale * jax.random.normal(own_key, shape, jnp.float32)
    if pieces:
        array = array * block_scale(own_key, shape, pieces, -0.22, 0.18)
    return jnp.clip(array, -bound, bound).astype(kind)


def setup_inputs(seed: int = 0) -> dict:
    streams_of = jax.random.split(jax.random.key(seed), 11)
    return {
        "x_vec": draw_x_vec(jax.random.fold_in(streams_of[10], 71), 0),
        "hx_vec": draw_hx_vec(jax.random.fold_in(streams_of[10], 71), 0),
        "p_vec": draw_p_vec(jax.random.fold_in(streams_of[10], 71), 0),
        "hp_vec": draw_hp_vec(jax.random.fold_in(streams_of[10], 71), 0),
        "theta": jnp.clip(jax.random.uniform(streams_of[4], (VECS,), jnp.float32, 0.5, 2.0), 0.5, 2.0),
        "precond": jnp.clip(jnp.exp(math.log(4.0) - 1.3862944 * jax.random.uniform(streams_of[5], (NDIM,), jnp.float32) ** block_scale(streams_of[5], (NDIM,), ((0, 128),), -0.2, 0.2)), 1.0, 4.0),
        "tile_vals": centred(streams_of[6], (N_ROW, N_COL, NZ, BLOCK * BLOCK), (2 * NZ * BLOCK * BLOCK // PIECE) ** -0.5, 0.25, ((0, 8), (1, 16))),
        "tile_rows": touch_ends(jax.random.randint(streams_of[7], (N_ROW, N_COL, NZ), 0, NBLK), jax.random.fold_in(streams_of[7], 1), 0, NBLK - 1).astype(jnp.int32),
        "tile_cols": touch_ends(jax.random.randint(streams_of[8], (N_ROW, N_COL, NZ), 0, NBLK), jax.random.fold_in(streams_of[8], 1), 0, NBLK - 1).astype(jnp.int32),
        "tile_count": draw_tile_count(jax.random.fold_in(streams_of[10], 71), 0),
    }


def segment_blocks(part, index, block_total):
    summed = jax.ops.segment_sum(part, index, num_segments=block_total)
    return jnp.transpose(summed, (1, 0, 2)).reshape(part.shape[1], -1)


def tile_terms(flat_values, row_index, col_index, live_mask, col_vec, row_vec):
    vec_count = col_vec.shape[0]
    values = flat_values.reshape(flat_values.shape[0], BLOCK, BLOCK)
    blocks_col = col_vec.reshape(vec_count, -1, BLOCK)
    blocks_row = row_vec.reshape(vec_count, -1, BLOCK)
    block_total = blocks_col.shape[1]
    picked_col = blocks_col[:, col_index, :].astype(jnp.float32)
    picked_row = blocks_row[:, row_index, :].astype(jnp.float32)
    wide = values.astype(jnp.float32)
    forward_part = jnp.einsum('zij,kzj->zki', wide, picked_col, precision=lax.Precision.HIGHEST) * live_mask[:, None, None]
    transpose_part = jnp.einsum('zij,kzi->zkj', wide, picked_row, precision=lax.Precision.HIGHEST) * live_mask[:, None, None]
    return segment_blocks(forward_part, row_index, block_total), segment_blocks(transpose_part, col_index, block_total)


def reference(x_vec, hx_vec, p_vec, hp_vec, theta, precond, tile_vals, tile_rows, tile_cols, tile_count):
    residue = (hx_vec - x_vec * theta[:, None]) / precond[None, :]
    w_send = residue.astype(jnp.bfloat16)
    seg_len = PIECE * N_ROW
    segments = w_send.reshape(VECS, N_COL, seg_len)

    def visit(tile_pos, accum):
        row_pos = tile_pos // N_COL
        col_pos = tile_pos % N_COL
        target = (col_pos + row_pos) % N_COL
        live_mask = (jnp.arange(NZ, dtype=jnp.int32) < tile_count[row_pos, col_pos]).astype(jnp.float32)
        forward_seg, transpose_seg = tile_terms(tile_vals[row_pos, col_pos], tile_rows[row_pos, col_pos], tile_cols[row_pos, col_pos], live_mask, segments[:, col_pos], segments[:, target])
        accum = accum.at[:, target].add(forward_seg)
        return accum.at[:, col_pos].add(transpose_seg)

    accum = lax.fori_loop(0, N_ROW * N_COL, visit, jnp.zeros((VECS, N_COL, seg_len), jnp.float32))
    hw_vec = accum.reshape(VECS, NDIM)
    vectors = jnp.concatenate([x_vec, residue, p_vec], 0)
    images = jnp.concatenate([hx_vec, hw_vec, hp_vec], 0)
    gram_a = jnp.dot(vectors, images.T, precision=lax.Precision.HIGHEST, preferred_element_type=jnp.float32) / NDIM
    gram_b = jnp.dot(vectors, vectors.T, precision=lax.Precision.HIGHEST, preferred_element_type=jnp.float32) / NDIM
    return hw_vec, gram_a, gram_b
```

```python
import functools

import jax
import jax.numpy as jnp
from jax import lax
from jax.experimental import pallas as pl
from jax.experimental.pallas import tpu as pltpu
from jax.sharding import PartitionSpec as P

BLOCK = 64
LANES = 128
BOTH = ("row", "col")
NT = (((1,), (1,)), ((), ()))
NN = (((1,), (0,)), ((), ()))


def one_hot(index, base, count):
    place = lax.broadcasted_iota(jnp.int32, (count, index.shape[1]), 0) + base
    return jnp.where(place == index, 1.0, 0.0).astype(jnp.bfloat16)


def gather_into(base_ref, index, piece_refs):
    total = None
    for d, piece in enumerate(piece_refs):
        hot = one_hot(index, base_ref[d], piece.shape[1])
        part = lax.dot_general(piece[...], hot, NN, preferred_element_type=jnp.float32)
        total = part if total is None else total + part
    return total


def pick_kernel(base_ref, index_ref, *refs):
    refs[-1][...] = gather_into(base_ref, index_ref[...], refs[:-1]).astype(jnp.bfloat16)


def pick(bases, index, pieces):
    slots = index.shape[1]
    return pl.pallas_call(
        pick_kernel,
        out_shape=jax.ShapeDtypeStruct((pieces[0].shape[0], slots), jnp.bfloat16),
        in_specs=[pl.BlockSpec(memory_space=pltpu.SMEM)]
        + [pl.BlockSpec(memory_space=pltpu.VMEM)] * (1 + len(pieces)),
        out_specs=pl.BlockSpec(memory_space=pltpu.VMEM),
        compiler_params=pltpu.CompilerParams(vmem_limit_bytes=40 << 20),
        name="pick",
    )(bases, index, *pieces)


def turned(tile, start, width):
    eye = (
        lax.broadcasted_iota(jnp.int32, (width, width), 0)
        == lax.broadcasted_iota(jnp.int32, (width, width), 1)
    )
    eye = jnp.where(eye, 1.0, 0.0).astype(jnp.bfloat16)
    return lax.dot_general(
        eye, tile[:, pl.ds(start, width)], NT, preferred_element_type=jnp.float32
    )


def fold8(parts):
    row = lax.broadcasted_iota(jnp.int32, parts[0].shape, 0)
    for half in (4, 2, 1):
        low = (row & half) == 0
        parts = [
            jnp.where(low, a, b) + pltpu.roll(jnp.where(low, b, a), half, 0)
            if half == 4
            else jnp.where(low, a + pltpu.roll(a, 8 - half, 0), b + pltpu.roll(b, half, 0))
            for a, b in zip(parts[: len(parts) // 2], parts[len(parts) // 2 :])
        ]
    return parts[0]


def forward_kernel(vecs, base_ref, index_ref, *refs):
    pieces, tile_ref, out_ref, x_ref = refs[:-3], refs[-3], refs[-2], refs[-1]
    x_ref[...] = gather_into(base_ref, index_ref[...], pieces)

    def step(g, _):
        for h in range(tile_ref.shape[0] // LANES):
            lanes = slice(h * LANES, (h + 1) * LANES)
            sums = [[] for _ in range(vecs)]
            for half in range(2):
                start = pl.multiple_of((g * 2 + half) * 4 * BLOCK, 4 * BLOCK)
                block = turned(tile_ref[lanes, pl.ds(start, 4 * BLOCK)], 0, 4 * BLOCK)
                for i in range(4):
                    line = block[i * BLOCK : (i + 1) * BLOCK]
                    for k in range(vecs):
                        prod = line * x_ref[k * BLOCK : (k + 1) * BLOCK, lanes]
                        sums[k].append(prod.reshape(BLOCK // 8, 8, LANES).sum(0))
            for k in range(vecs):
                at = pl.multiple_of(k * BLOCK + g * 8, 8)
                out_ref[pl.ds(at, 8), lanes] = fold8(sums[k])
        return 0

    lax.fori_loop(0, BLOCK // 8, step, 0)


def forward(vecs, bases, index, pieces, tile):
    slots, width = tile.shape
    step = 256
    whole = pl.BlockSpec(memory_space=pltpu.VMEM)
    return pl.pallas_call(
        functools.partial(forward_kernel, vecs),
        grid=(slots // step,),
        out_shape=jax.ShapeDtypeStruct((vecs * BLOCK, slots), jnp.float32),
        in_specs=[pl.BlockSpec(memory_space=pltpu.SMEM), pl.BlockSpec((1, step), lambda i: (0, i))]
        + [whole] * len(pieces)
        + [pl.BlockSpec((step, width), lambda i: (i, 0))],
        out_specs=pl.BlockSpec((vecs * BLOCK, step), lambda i: (0, i)),
        scratch_shapes=[pltpu.VMEM((vecs * BLOCK, step), jnp.float32)],
        compiler_params=pltpu.CompilerParams(vmem_limit_bytes=40 << 20),
        name="forward",
    )(bases, index, *pieces, tile)


def backward_kernel(vecs, y_ref, tile_ref, high_ref, low_ref, y32_ref, sum_ref):
    y32_ref[...] = y_ref[...].astype(jnp.float32)
    sum_ref[...] = jnp.zeros_like(sum_ref)

    def step(g, _):
        for h in range(tile_ref.shape[0] // LANES):
            lanes = slice(h * LANES, (h + 1) * LANES)
            weights = [y32_ref[pl.ds(pl.multiple_of(k * BLOCK + g * 8, 8), 8), lanes] for k in range(vecs)]
            for half in range(2):
                start = pl.multiple_of((g * 2 + half) * 4 * BLOCK, 4 * BLOCK)
                block = turned(tile_ref[lanes, pl.ds(start, 4 * BLOCK)], 0, 4 * BLOCK)
                for k in range(vecs):
                    rows = slice(k * BLOCK, (k + 1) * BLOCK)
                    total = sum_ref[rows, lanes]
                    for i in range(4):
                        weight = weights[k][half * 4 + i : half * 4 + i + 1]
                        total = total + block[i * BLOCK : (i + 1) * BLOCK] * weight
                    sum_ref[rows, lanes] = total
        return 0

    lax.fori_loop(0, BLOCK // 8, step, 0)
    total = sum_ref[...]
    high = total.astype(jnp.bfloat16)
    high_ref[...] = high
    low_ref[...] = (total - high.astype(jnp.float32)).astype(jnp.bfloat16)


def backward(vecs, far, tile):
    slots, width = tile.shape
    step = 256
    column = pl.BlockSpec((vecs * BLOCK, step), lambda i: (0, i))
    shape = jax.ShapeDtypeStruct((vecs * BLOCK, slots), jnp.bfloat16)
    return pl.pallas_call(
        functools.partial(backward_kernel, vecs),
        grid=(slots // step,),
        out_shape=(shape, shape),
        in_specs=[column, pl.BlockSpec((step, width), lambda i: (i, 0))],
        out_specs=(column, column),
        scratch_shapes=[pltpu.VMEM((vecs * BLOCK, step), jnp.float32)] * 2,
        compiler_params=pltpu.CompilerParams(vmem_limit_bytes=40 << 20),
        name="backward",
    )(far, tile)


def spread_kernel(col_ref, row_ref, high_ref, low_ref, forth_ref, out_ref):
    width = out_ref.shape[2]
    base = pl.program_id(0) * width
    hot = one_hot(col_ref[...], base, width)
    total = lax.dot_general(high_ref[...], hot, NT, preferred_element_type=jnp.float32)
    total += lax.dot_general(low_ref[...], hot, NT, preferred_element_type=jnp.float32)
    hot = one_hot(row_ref[...], base, width)
    total += lax.dot_general(forth_ref[...], hot, NT, preferred_element_type=jnp.float32)
    out_ref[0] = total.astype(jnp.bfloat16)


def spread(col_index, row_index, high, low, forth, count, width):
    whole = pl.BlockSpec(memory_space=pltpu.VMEM)
    return pl.pallas_call(
        spread_kernel,
        grid=(count,),
        out_shape=jax.ShapeDtypeStruct((count, high.shape[0], width), jnp.bfloat16),
        in_specs=[whole] * 5,
        out_specs=pl.BlockSpec((1, high.shape[0], width), lambda i: (i, 0, 0)),
        compiler_params=pltpu.CompilerParams(vmem_limit_bytes=40 << 20),
        name="spread",
    )(col_index, row_index, high, low, forth)


def body(x_vec, hx_vec, p_vec, hp_vec, theta, precond, tile_vals, tile_rows, tile_cols, tile_count):
    vecs, piece_len = x_vec.shape
    rows, cols = lax.axis_size("row"), lax.axis_size("col")
    ndim_total = piece_len * rows * cols
    row_pos = lax.axis_index("row")
    width = piece_len // BLOCK
    slots = tile_vals.shape[2]
    tile = tile_vals[0, 0]
    residue = (hx_vec - x_vec * theta[:, None]) / precond[None, :]
    live = jnp.arange(slots, dtype=jnp.int32) < tile_count[0, 0]
    row_index = jnp.where(live, tile_rows[0, 0], -1)[None]
    col_index = jnp.where(live, tile_cols[0, 0], -1)[None]

    def along(block, sign):
        route = [(r * cols + c, r * cols + (c + sign * r) % cols) for r in range(rows) for c in range(cols)]
        return lax.ppermute(block, BOTH, route)

    far_index = along(row_index, 1)
    turned_piece = (
        residue.astype(jnp.bfloat16).reshape(vecs, width, BLOCK).transpose(0, 2, 1).reshape(vecs * BLOCK, width)
    )
    pieces = [turned_piece]
    for d in range(1, rows):
        pieces.append(lax.ppermute(turned_piece, "row", [(i, (i + d) % rows) for i in range(rows)]))
    bases = width * ((row_pos - jnp.arange(rows, dtype=jnp.int32)) % rows)
    far = along(pick(bases, far_index, pieces), -1)
    forth = along(forward(vecs, bases, col_index, pieces, tile).astype(jnp.bfloat16), 1)
    high, low = backward(vecs, far, tile)
    parts = spread(col_index, far_index, high, low, forth, rows, width)
    parts = lax.all_to_all(parts, "row", 0, 0, tiled=True)
    total = parts.astype(jnp.float32).sum(0)
    hw_vec = total.reshape(vecs, BLOCK, width).transpose(0, 2, 1).reshape(vecs, piece_len)

    vectors = jnp.concatenate([x_vec, residue, p_vec], 0)
    known = jnp.concatenate([vectors, hx_vec, hp_vec], 0)
    early = jnp.dot(vectors, known.T, precision=lax.Precision.HIGHEST, preferred_element_type=jnp.float32)
    late = jnp.dot(vectors, hw_vec.T, precision=lax.Precision.HIGHEST, preferred_element_type=jnp.float32)
    gram = jnp.concatenate([early, late], 1)
    flat = jnp.pad(gram.reshape(-1), (0, 3 * LANES - gram.size)).reshape(1, 3, LANES)
    flat = jnp.broadcast_to(flat, (rows * cols, 3, LANES))
    gram = lax.all_to_all(flat, BOTH, 0, 0, tiled=True).sum(0).reshape(-1)[: gram.size].reshape(gram.shape)
    gram = gram / ndim_total
    n = 3 * vecs
    gram_a = jnp.concatenate([gram[:, n : n + vecs], gram[:, n + 2 * vecs :], gram[:, n + vecs : n + 2 * vecs]], 1)
    return hw_vec, gram_a, gram[:, :n]


def solution(mesh):
    vector = P(None, ("col", "row"))
    placed = (
        vector,
        vector,
        vector,
        vector,
        P(),
        P(("col", "row")),
        P("row", "col", None, None),
        P("row", "col", None),
        P("row", "col", None),
        P("row", "col"),
    )
    return jax.shard_map(body, mesh=mesh, in_specs=placed, out_specs=(vector, P(), P()), check_vma=False)
```

```python
import functools
import jax
import jax.numpy as jnp
import numpy as np
from jax import lax
from jax.experimental import pallas as pl
from jax.experimental.pallas import tpu as pltpu
from jax.sharding import PartitionSpec as P

BLOCK = 64
LANES = 128
PAIRS = BLOCK * BLOCK // LANES
GROUP = 16
HALF = PAIRS // 2
SIZE = PAIRS * GROUP
STEP = 512
BOTH = ("row", "col")
NT = (((1,), (1,)), ((), ()))
NN = (((1,), (0,)), ((), ()))
F32 = jnp.float32
BF16 = jnp.bfloat16


def params(mib):
    return pltpu.CompilerParams(vmem_limit_bytes=mib << 20)


def dot(a, b, dims=NN):
    return lax.dot_general(a, b, dims, preferred_element_type=F32)


def as_ones(mask):
    return jnp.where(mask, 1.0, 0.0).astype(BF16)


def gathered(base_ref, index, piece_refs):
    shape = (index.shape[0], piece_refs[0].shape[0])
    place = jnp.broadcast_to(index, shape) - lax.broadcasted_iota(jnp.int32, shape, 1)
    total = None
    for d, piece in enumerate(piece_refs):
        part = dot(as_ones(place == base_ref[d]), piece[...])
        total = part if total is None else total + part
    return total


def pick_kernel(base_ref, index_ref, *refs):
    refs[-1][...] = gathered(base_ref, index_ref[...], refs[:-1]).astype(BF16)


def pick(bases, index, pieces):
    slots, step = index.shape[0], 256
    whole = pl.BlockSpec(memory_space=pltpu.VMEM)
    return pl.pallas_call(
        pick_kernel,
        grid=(slots // step,),
        out_shape=jax.ShapeDtypeStruct((slots, pieces[0].shape[1]), BF16),
        in_specs=[pl.BlockSpec(memory_space=pltpu.SMEM), pl.BlockSpec((step, 1), lambda i: (i, 0))]
        + [whole] * len(pieces),
        out_specs=pl.BlockSpec((step, pieces[0].shape[1]), lambda i: (i, 0)),
        compiler_params=params(12),
        name="pick",
    )(bases, index, *pieces)


def route_matrix(vecs):
    row = np.arange(2 * vecs * SIZE)[:, None]
    kind, pair = row // SIZE, row % SIZE // GROUP
    return jnp.asarray(np.arange(vecs * BLOCK) == kind // 2 * BLOCK + 2 * pair + kind % 2, BF16)


def own_mask(rows):
    shape = (rows, SIZE)
    return (
        lax.broadcasted_iota(jnp.int32, shape, 1) % GROUP == lax.broadcasted_iota(jnp.int32, shape, 0) % GROUP
    )


def stacked(tile_ref, at, half):
    parts = [tile_ref[at, c * LANES : (c + 1) * LANES] for c in range(half * HALF, (half + 1) * HALF)]
    return jnp.concatenate(parts, 0)


def forward_kernel(vecs, base_ref, index_ref, *refs):
    pieces, (route_ref, tile_ref, out_ref, x_ref, wide_ref) = refs[:-5], refs[-5:]
    x_ref[...] = gathered(base_ref, index_ref[...], pieces)
    first = lax.broadcasted_iota(jnp.int32, (GROUP, LANES), 1) < BLOCK
    own = own_mask(GROUP)
    span = HALF * GROUP

    def step(g, _):
        at = pl.ds(pl.multiple_of(g * GROUP, GROUP), GROUP)
        rows = []
        for p in range(vecs // 2):
            both = x_ref[at, p * LANES : (p + 1) * LANES]
            swapped = pltpu.roll(both, BLOCK, 1)
            rows += [
                jnp.where(first, both, 0.0),
                jnp.where(first, 0.0, swapped),
                jnp.where(first, swapped, 0.0),
                jnp.where(first, 0.0, both),
            ]
        left = jnp.concatenate(rows, 0).astype(BF16)
        for half in range(2):
            out = dot(left, stacked(tile_ref, at, half), NT)
            for s in range(2 * vecs):
                part = jnp.where(own[:, :span], out[s * GROUP : (s + 1) * GROUP], 0.0)
                wide_ref[at, s * SIZE + half * span : s * SIZE + (half + 1) * span] = part.astype(BF16)
        return 0

    lax.fori_loop(0, x_ref.shape[0] // GROUP, step, 0, unroll=8)
    out_ref[...] = dot(wide_ref[...], route_ref[...]).astype(BF16)


def forward(vecs, bases, index, pieces, route, tile):
    slots, size = tile.shape
    wide = vecs * BLOCK
    whole = pl.BlockSpec(memory_space=pltpu.VMEM)
    return pl.pallas_call(
        functools.partial(forward_kernel, vecs),
        grid=(slots // STEP,),
        out_shape=jax.ShapeDtypeStruct((slots, wide), BF16),
        in_specs=[pl.BlockSpec(memory_space=pltpu.SMEM), pl.BlockSpec((STEP, 1), lambda i: (i, 0))]
        + [whole] * (len(pieces) + 1)
        + [pl.BlockSpec((STEP, size), lambda i: (i, 0))],
        out_specs=pl.BlockSpec((STEP, wide), lambda i: (i, 0)),
        scratch_shapes=[pltpu.VMEM((STEP, wide), F32), pltpu.VMEM((STEP, 2 * vecs * SIZE), BF16)],
        compiler_params=params(28),
        name="forward",
    )(bases, index, *pieces, route, tile)


def backward_kernel(vecs, y_ref, route_ref, tile_ref, out_ref, wide_ref):
    own = own_mask(y_ref.shape[0])
    for s in range(2 * vecs):
        part = dot(y_ref[...], route_ref[s * SIZE : (s + 1) * SIZE, :], NT)
        wide_ref[:, s * SIZE : (s + 1) * SIZE] = jnp.where(own, part, 0.0).astype(BF16)
    first = lax.broadcasted_iota(jnp.int32, (GROUP, LANES), 1) < BLOCK
    span = HALF * GROUP

    def step(g, _):
        at = pl.ds(pl.multiple_of(g * GROUP, GROUP), GROUP)
        out = None
        for half in range(2):
            left = [
                wide_ref[at, s * SIZE + half * span : s * SIZE + (half + 1) * span] for s in range(2 * vecs)
            ]
            part = dot(jnp.concatenate(left, 0), stacked(tile_ref, at, half))
            out = part if out is None else out + part
        sums = []
        for k in range(vecs):
            even, odd = out[2 * k * GROUP : (2 * k + 1) * GROUP], out[(2 * k + 1) * GROUP : (2 * k + 2) * GROUP]
            part = jnp.where(first, even, odd)
            sums.append(part + pltpu.roll(part, BLOCK, 1))
        for p in range(vecs // 2):
            out_ref[at, p * LANES : (p + 1) * LANES] = jnp.where(first, sums[2 * p], sums[2 * p + 1]).astype(BF16)
        return 0

    lax.fori_loop(0, y_ref.shape[0] // GROUP, step, 0, unroll=8)


def backward(vecs, far, route, tile):
    slots, wide = far.shape
    block = pl.BlockSpec((STEP, wide), lambda i: (i, 0))
    return pl.pallas_call(
        functools.partial(backward_kernel, vecs),
        grid=(slots // STEP,),
        out_shape=jax.ShapeDtypeStruct((slots, wide), BF16),
        in_specs=[
            block,
            pl.BlockSpec(memory_space=pltpu.VMEM),
            pl.BlockSpec((STEP, tile.shape[1]), lambda i: (i, 0)),
        ],
        out_specs=block,
        scratch_shapes=[pltpu.VMEM((STEP, 2 * vecs * SIZE), BF16)],
        compiler_params=params(28),
        name="backward",
    )(far, route, tile)


def spread_kernel(col_ref, row_ref, back_ref, forth_ref, out_ref):
    count = out_ref.shape[1]
    place = lax.broadcasted_iota(jnp.int32, (count, col_ref.shape[1]), 0) + pl.program_id(0) * count
    total = dot(as_ones(place == col_ref[...]), back_ref[...])
    total += dot(as_ones(place == row_ref[...]), forth_ref[...])
    out_ref[0] = total.astype(BF16)


def spread(col_index, row_index, back, forth, count, width):
    whole = pl.BlockSpec(memory_space=pltpu.VMEM)
    return pl.pallas_call(
        spread_kernel,
        grid=(count,),
        out_shape=jax.ShapeDtypeStruct((count, width, back.shape[1]), BF16),
        in_specs=[whole] * 4,
        out_specs=pl.BlockSpec((1, width, back.shape[1]), lambda i: (i, 0, 0)),
        compiler_params=params(16),
        name="spread",
    )(col_index, row_index, back, forth)


def body(x_vec, hx_vec, p_vec, hp_vec, theta, precond, tile_vals, tile_rows, tile_cols, tile_count):
    vecs, piece_len = x_vec.shape
    rows, cols = lax.axis_size("row"), lax.axis_size("col")
    ring = rows // 2
    ndim_total = piece_len * rows * cols
    row_pos = lax.axis_index("row")
    width = piece_len // BLOCK
    slots = tile_vals.shape[2]
    tile = tile_vals[0, 0]
    route = route_matrix(vecs)
    residue = (hx_vec - x_vec * theta[:, None]) / precond[None, :]
    live = jnp.arange(slots, dtype=jnp.int32) < tile_count[0, 0]
    row_index = jnp.where(live, tile_rows[0, 0], -1)[None]
    col_index = jnp.where(live, tile_cols[0, 0], -1)[None]

    def along(block, sign):
        path = [(r * cols + c, r * cols + (c + sign * r) % cols) for r in range(rows) for c in range(cols)]
        return lax.ppermute(block, BOTH, path)

    def within(block, flip, turn):
        return lax.ppermute(
            block, "row", [(i, (i // ring ^ flip) * ring + (i % ring + turn) % ring) for i in range(rows)]
        )

    own = residue.astype(BF16).reshape(vecs, width, BLOCK).transpose(1, 0, 2).reshape(width, vecs * BLOCK)
    offsets = [(0, 0), (1, 0), (0, 1), (0, 3), (1, 1), (1, 3), (0, 2), (1, 2)]
    pieces = [own] + [within(own, *o) for o in offsets[1:]]
    flips = jnp.array([o[0] for o in offsets], jnp.int32)
    turns = jnp.array([o[1] for o in offsets], jnp.int32)
    bases = width * ((row_pos // ring ^ flips) * ring + (row_pos % ring - turns) % ring)
    far_index = along(row_index, 1)
    far = along(pick(bases, far_index.reshape(slots, 1), pieces), -1)
    forth = along(forward(vecs, bases, col_index.reshape(slots, 1), pieces, route, tile), 1)
    back = backward(vecs, far, route, tile)
    parts = spread(col_index, far_index, back, forth, rows, width)
    parts = lax.all_to_all(parts, "row", 0, 0, tiled=True)
    total = parts.astype(F32).sum(0)
    hw_vec = total.reshape(width, vecs, BLOCK).transpose(1, 0, 2).reshape(vecs, piece_len)

    vectors = jnp.concatenate([x_vec, residue, p_vec], 0)
    known = jnp.concatenate([vectors, hx_vec, hp_vec], 0)
    early = jnp.dot(vectors, known.T, precision=lax.Precision.HIGHEST, preferred_element_type=jnp.float32)
    late = jnp.dot(vectors, hw_vec.T, precision=lax.Precision.HIGHEST, preferred_element_type=jnp.float32)
    gram = jnp.concatenate([early, late], 1)
    flat = jnp.pad(gram.reshape(-1), (0, 3 * LANES - gram.size)).reshape(1, 3, LANES)
    flat = jnp.broadcast_to(flat, (rows * cols, 3, LANES))
    gram = lax.all_to_all(flat, BOTH, 0, 0, tiled=True).sum(0).reshape(-1)[: gram.size].reshape(gram.shape)
    gram = gram / ndim_total
    n = 3 * vecs
    gram_a = jnp.concatenate([gram[:, n : n + vecs], gram[:, n + 2 * vecs :], gram[:, n + vecs : n + 2 * vecs]], 1)
    return hw_vec, gram_a, gram[:, :n]


def solution(mesh):
    vector = P(None, ("col", "row"))
    placed = (
        vector,
        vector,
        vector,
        vector,
        P(),
        P(("col", "row")),
        P("row", "col", None, None),
        P("row", "col", None),
        P("row", "col", None),
        P("row", "col"),
    )
    return jax.shard_map(body, mesh=mesh, in_specs=placed, out_specs=(vector, P(), P()), check_vma=False)
```

```python
import functools
import jax
import jax.numpy as jnp
import numpy as np
from jax import lax
from jax.experimental import pallas as pl
from jax.experimental.pallas import tpu as pltpu
from jax.sharding import PartitionSpec as P

BLOCK = 64
LANES = 128
PAIRS = BLOCK * BLOCK // LANES
GROUP = 16
HALF = PAIRS // 2
SIZE = PAIRS * GROUP
STEP = 512
BOTH = ("row", "col")
NT = (((1,), (1,)), ((), ()))
NN = (((1,), (0,)), ((), ()))
F32 = jnp.float32
BF16 = jnp.bfloat16


def params(mib):
    return pltpu.CompilerParams(vmem_limit_bytes=mib << 20)


def dot(a, b, dims=NN):
    return lax.dot_general(a, b, dims, preferred_element_type=F32)


def as_ones(mask):
    return jnp.where(mask, 1.0, 0.0).astype(BF16)


def gathered(base_ref, index, piece_refs):
    shape = (piece_refs[0].shape[1], index.shape[1])
    place = index - lax.broadcasted_iota(jnp.int32, shape, 0)
    total = None
    for d, piece in enumerate(piece_refs):
        part = dot(piece[...], as_ones(place == base_ref[d]))
        total = part if total is None else total + part
    return total


def pick_kernel(base_ref, index_ref, *refs):
    refs[-1][...] = gathered(base_ref, index_ref[...], refs[:-1]).astype(BF16)


def pick(bases, index, pieces):
    whole = pl.BlockSpec(memory_space=pltpu.VMEM)
    return pl.pallas_call(
        pick_kernel,
        out_shape=jax.ShapeDtypeStruct((pieces[0].shape[0], index.shape[1]), BF16),
        in_specs=[pl.BlockSpec(memory_space=pltpu.SMEM)] + [whole] * (1 + len(pieces)),
        out_specs=whole,
        compiler_params=params(16),
        name="pick",
    )(bases, index, *pieces)


def route_matrix(vecs):
    row = np.arange(2 * vecs * SIZE)[:, None]
    kind, pair = row // SIZE, row % SIZE // GROUP
    return jnp.asarray(np.arange(vecs * BLOCK) == kind // 2 * BLOCK + 2 * pair + kind % 2, BF16)


def own_mask(rows):
    shape = (rows, SIZE)
    return (
        lax.broadcasted_iota(jnp.int32, shape, 1) % GROUP == lax.broadcasted_iota(jnp.int32, shape, 0) % GROUP
    )


def stacked(tile_ref, at, half):
    parts = [tile_ref[at, c * LANES : (c + 1) * LANES] for c in range(half * HALF, (half + 1) * HALF)]
    return jnp.concatenate(parts, 0)


def forward_kernel(vecs, base, base_ref, index_ref, *refs):
    pieces, (route_ref, tile_ref, out_ref, x_ref, wide_ref) = refs[:-5], refs[-5:]
    x_ref[...] = gathered(base_ref, index_ref[...], pieces).T
    first = lax.broadcasted_iota(jnp.int32, (GROUP, LANES), 1) < BLOCK
    own = own_mask(GROUP)
    span = HALF * GROUP

    def step(g, _):
        at = pl.ds(pl.multiple_of(g * GROUP, GROUP), GROUP)
        start = pl.ds(pl.multiple_of(base + g * GROUP, GROUP), GROUP)
        rows = []
        for p in range(vecs // 2):
            both = x_ref[at, p * LANES : (p + 1) * LANES]
            swapped = pltpu.roll(both, BLOCK, 1)
            rows += [
                jnp.where(first, both, 0.0),
                jnp.where(first, 0.0, swapped),
                jnp.where(first, swapped, 0.0),
                jnp.where(first, 0.0, both),
            ]
        left = jnp.concatenate(rows, 0).astype(BF16)
        for half in range(2):
            out = dot(left, stacked(tile_ref, start, half), NT)
            for s in range(2 * vecs):
                part = jnp.where(own[:, :span], out[s * GROUP : (s + 1) * GROUP], 0.0)
                wide_ref[at, s * SIZE + half * span : s * SIZE + (half + 1) * span] = part.astype(BF16)
        return 0

    lax.fori_loop(0, x_ref.shape[0] // GROUP, step, 0, unroll=8)
    out_ref[...] = dot(wide_ref[...], route_ref[...]).astype(BF16)


def forward(vecs, bases, index, pieces, route, tile, at):
    wide = vecs * BLOCK
    whole = pl.BlockSpec(memory_space=pltpu.VMEM)
    return pl.pallas_call(
        functools.partial(forward_kernel, vecs, at * STEP),
        grid=(1,),
        out_shape=jax.ShapeDtypeStruct((STEP, wide), BF16),
        in_specs=[pl.BlockSpec(memory_space=pltpu.SMEM), pl.BlockSpec((1, STEP), lambda i: (0, at))]
        + [whole] * (len(pieces) + 2),
        out_specs=whole,
        scratch_shapes=[pltpu.VMEM((STEP, wide), F32), pltpu.VMEM((STEP, 2 * vecs * SIZE), BF16)],
        compiler_params=params(20),
        name="forward",
    )(bases, index, *pieces, route, tile)


def backward_kernel(vecs, y_ref, route_ref, tile_ref, out_ref, wide_ref):
    own = own_mask(out_ref.shape[0])
    far = y_ref[...].astype(F32).T.astype(BF16)
    for s in range(2 * vecs):
        part = dot(far, route_ref[s * SIZE : (s + 1) * SIZE, :], NT)
        wide_ref[:, s * SIZE : (s + 1) * SIZE] = jnp.where(own, part, 0.0).astype(BF16)
    first = lax.broadcasted_iota(jnp.int32, (GROUP, LANES), 1) < BLOCK
    span = HALF * GROUP

    def step(g, _):
        at = pl.ds(pl.multiple_of(g * GROUP, GROUP), GROUP)
        out = None
        for half in range(2):
            left = [
                wide_ref[at, s * SIZE + half * span : s * SIZE + (half + 1) * span] for s in range(2 * vecs)
            ]
            part = dot(jnp.concatenate(left, 0), stacked(tile_ref, at, half))
            out = part if out is None else out + part
        sums = []
        for k in range(vecs):
            even, odd = out[2 * k * GROUP : (2 * k + 1) * GROUP], out[(2 * k + 1) * GROUP : (2 * k + 2) * GROUP]
            part = jnp.where(first, even, odd)
            sums.append(part + pltpu.roll(part, BLOCK, 1))
        for p in range(vecs // 2):
            out_ref[at, p * LANES : (p + 1) * LANES] = jnp.where(first, sums[2 * p], sums[2 * p + 1]).astype(BF16)
        return 0

    lax.fori_loop(0, out_ref.shape[0] // GROUP, step, 0, unroll=8)


def backward(vecs, far, route, tile):
    wide, slots = far.shape
    whole = pl.BlockSpec(memory_space=pltpu.VMEM)
    return pl.pallas_call(
        functools.partial(backward_kernel, vecs),
        out_shape=jax.ShapeDtypeStruct((slots, wide), BF16),
        in_specs=[whole] * 3,
        out_specs=whole,
        scratch_shapes=[pltpu.VMEM((slots, 2 * vecs * SIZE), BF16)],
        compiler_params=params(20),
        name="backward",
    )(far, route, tile)


def spread_kernel(col_ref, row_ref, back_ref, *refs):
    forth_refs, out_ref = refs[:-1], refs[-1]
    count = out_ref.shape[1]
    place = lax.broadcasted_iota(jnp.int32, (count, col_ref.shape[1]), 0) + pl.program_id(0) * count
    total = dot(as_ones(place == col_ref[...]), back_ref[...])
    hot = as_ones(place == row_ref[...])
    for n, forth in enumerate(forth_refs):
        total += dot(hot[:, n * STEP : (n + 1) * STEP], forth[...])
    out_ref[0] = total.astype(BF16)


def spread(col_index, row_index, back, forth, count, width):
    whole = pl.BlockSpec(memory_space=pltpu.VMEM)
    return pl.pallas_call(
        spread_kernel,
        grid=(count,),
        out_shape=jax.ShapeDtypeStruct((count, width, back.shape[1]), BF16),
        in_specs=[whole] * (3 + len(forth)),
        out_specs=pl.BlockSpec((1, width, back.shape[1]), lambda i: (i, 0, 0)),
        compiler_params=params(16),
        name="spread",
    )(col_index, row_index, back, *forth)


def body(x_vec, hx_vec, p_vec, hp_vec, theta, precond, tile_vals, tile_rows, tile_cols, tile_count):
    vecs, piece_len = x_vec.shape
    rows, cols = lax.axis_size("row"), lax.axis_size("col")
    ring = rows // 2
    ndim_total = piece_len * rows * cols
    row_pos = lax.axis_index("row")
    width = piece_len // BLOCK
    slots = tile_vals.shape[2]
    tile = tile_vals[0, 0]
    route = route_matrix(vecs)
    residue = (hx_vec - x_vec * theta[:, None]) / precond[None, :]
    live = jnp.arange(slots, dtype=jnp.int32) < tile_count[0, 0]
    row_index = jnp.where(live, tile_rows[0, 0], -1)[None]
    col_index = jnp.where(live, tile_cols[0, 0], -1)[None]

    def along(block, sign):
        path = [(r * cols + c, r * cols + (c + sign * r) % cols) for r in range(rows) for c in range(cols)]
        return lax.ppermute(block, BOTH, path)

    def within(block, flip, turn):
        return lax.ppermute(
            block, "row", [(i, (i // ring ^ flip) * ring + (i % ring + turn) % ring) for i in range(rows)]
        )

    own = residue.astype(BF16).reshape(vecs, width, BLOCK).transpose(0, 2, 1).reshape(vecs * BLOCK, width)
    offsets = [(0, 0), (1, 0), (0, 1), (0, 3), (1, 1), (1, 3), (0, 2), (1, 2)]
    pieces = [own] + [within(own, *o) for o in offsets[1:]]
    flips = jnp.array([o[0] for o in offsets], jnp.int32)
    turns = jnp.array([o[1] for o in offsets], jnp.int32)
    bases = width * ((row_pos // ring ^ flips) * ring + (row_pos % ring - turns) % ring)
    far_index = along(lax.optimization_barrier((row_index, pieces[3]))[0], 1)
    far = along(pick(bases, far_index, pieces), -1)
    forth = [
        along(forward(vecs, bases, col_index, pieces, route, tile, n), 1) for n in range(slots // STEP)
    ]
    back = backward(vecs, far, route, tile)
    parts = spread(col_index, far_index, back, forth, rows, width)
    parts = lax.all_to_all(parts, "row", 0, 0, tiled=True)
    total = parts.astype(F32).sum(0)
    hw_vec = total.reshape(width, vecs, BLOCK).transpose(1, 0, 2).reshape(vecs, piece_len)

    vectors = jnp.concatenate([x_vec, residue, p_vec], 0)
    known = jnp.concatenate([vectors, hx_vec, hp_vec], 0)
    early = jnp.dot(vectors, known.T, precision=lax.Precision.HIGHEST, preferred_element_type=jnp.float32)
    late = jnp.dot(vectors, hw_vec.T, precision=lax.Precision.HIGHEST, preferred_element_type=jnp.float32)
    gram = jnp.concatenate([early, late], 1)
    flat = jnp.pad(gram.reshape(-1), (0, 3 * LANES - gram.size)).reshape(1, 3, LANES)
    flat = jnp.broadcast_to(flat, (rows * cols, 3, LANES))
    gram = lax.all_to_all(flat, BOTH, 0, 0, tiled=True).sum(0).reshape(-1)[: gram.size].reshape(gram.shape)
    gram = gram / ndim_total
    n = 3 * vecs
    gram_a = jnp.concatenate([gram[:, n : n + vecs], gram[:, n + 2 * vecs :], gram[:, n + vecs : n + 2 * vecs]], 1)
    return hw_vec, gram_a, gram[:, :n]


def solution(mesh):
    vector = P(None, ("col", "row"))
    placed = (
        vector,
        vector,
        vector,
        vector,
        P(),
        P(("col", "row")),
        P("row", "col", None, None),
        P("row", "col", None),
        P("row", "col", None),
        P("row", "col"),
    )
    return jax.shard_map(body, mesh=mesh, in_specs=placed, out_specs=(vector, P(), P()), check_vma=False)
```

```python
import functools

import jax
import jax.numpy as jnp
import numpy as np
from jax import lax
from jax.experimental import pallas as pl
from jax.experimental.pallas import tpu as pltpu
from jax.sharding import PartitionSpec as P

BLOCK = 64
LANES = 128
PAIRS = BLOCK * BLOCK // LANES
GROUP = 16
HALF = PAIRS // 2
SIZE = PAIRS * GROUP
WIDTH = 1024
BOTH = ("row", "col")
NT = (((1,), (1,)), ((), ()))
NN = (((1,), (0,)), ((), ()))
F32 = jnp.float32
BF16 = jnp.bfloat16


def params(mib):
    return pltpu.CompilerParams(vmem_limit_bytes=mib << 20)


def dot(a, b, dims=NN):
    return lax.dot_general(a, b, dims, preferred_element_type=F32)


def as_ones(mask):
    return jnp.where(mask, 1.0, 0.0).astype(BF16)


def gathered(base_ref, index, piece_refs):
    shape = (piece_refs[0].shape[1], index.shape[1])
    place = index - lax.broadcasted_iota(jnp.int32, shape, 0)
    total = None
    for d, piece in enumerate(piece_refs):
        part = dot(piece[...], as_ones(place == base_ref[d]))
        total = part if total is None else total + part
    return total


def pick_kernel(base_ref, index_ref, *refs):
    pieces, (out_ref, turned_ref) = refs[:-2], refs[-2:]
    turned_ref[...] = turned_slots(index_ref[...])
    out_ref[...] = gathered(base_ref, index_ref[...], pieces).astype(BF16)


def pick(bases, index, pieces):
    whole = pl.BlockSpec(memory_space=pltpu.VMEM)
    return pl.pallas_call(
        pick_kernel,
        out_shape=(
            jax.ShapeDtypeStruct((pieces[0].shape[0], index.shape[1]), BF16),
            jax.ShapeDtypeStruct(index.shape, index.dtype),
        ),
        in_specs=[pl.BlockSpec(memory_space=pltpu.SMEM)] + [whole] * (1 + len(pieces)),
        out_specs=(whole, whole),
        compiler_params=params(16),
        name="pick",
    )(bases, index, *pieces)


def order_matrix(vecs):
    place = np.arange(vecs * BLOCK)
    pair, kind = place // GROUP, place % GROUP
    half, k, parity = kind // (2 * vecs), kind % (2 * vecs) // 2, kind % 2
    entry = k * BLOCK + 2 * (half * HALF + pair) + parity
    return jnp.asarray(np.arange(vecs * BLOCK)[:, None] == entry, BF16)


def route_matrix(vecs):
    row = np.arange(2 * vecs * SIZE)[:, None]
    kind, pair = row // SIZE, row % SIZE // GROUP
    return jnp.asarray(np.arange(vecs * BLOCK) == kind // 2 * BLOCK + 2 * pair + kind % 2, BF16)


def turned_slots(index):
    lane = lax.broadcasted_iota(jnp.int32, (1, LANES), 1)
    parts = []
    for n in range(index.shape[1] // LANES):
        part = index[:, n * LANES : (n + 1) * LANES]
        for bit in (1, 2, 4, 8):
            part = jnp.where(lane & bit != 0, pltpu.roll(part, bit, 1), pltpu.roll(part, LANES - bit, 1))
        parts.append(part)
    return jnp.concatenate(parts, 1)


def stage_kernel(tile_ref, out_ref, sem):
    copy = pltpu.make_async_copy(tile_ref, out_ref, sem)
    copy.start()
    copy.wait()


def stage(tile):
    return pl.pallas_call(
        stage_kernel,
        out_shape=jax.ShapeDtypeStruct(tile.shape, tile.dtype),
        in_specs=[pl.BlockSpec(memory_space=pl.ANY)],
        out_specs=pl.BlockSpec(memory_space=pltpu.VMEM),
        scratch_shapes=[pltpu.SemaphoreType.DMA],
        compiler_params=params(12),
        name="stage",
    )(tile)


def stacked(tile_ref, at, half):
    parts = [tile_ref[at, c * LANES : (c + 1) * LANES] for c in range(half * HALF, (half + 1) * HALF)]
    return jnp.concatenate(parts, 0)


def forward_kernel(vecs, base_ref, index_ref, *refs):
    pieces, (order_ref, tile_ref, out_ref, x_ref, packed_ref) = refs[:-5], refs[-5:]
    x_ref[...] = gathered(base_ref, turned_slots(index_ref[...]), pieces).T
    lane = lax.broadcasted_iota(jnp.int32, (GROUP, LANES), 1)
    row = lax.broadcasted_iota(jnp.int32, (GROUP, LANES), 0)
    first = lane < BLOCK
    masks = [as_ones((lane + row + 1) % GROUP == n) for n in range(GROUP)]

    def step(g, _):
        at = pl.ds(pl.multiple_of(g * GROUP, GROUP), GROUP)
        rows = []
        for p in range(vecs // 2):
            both = x_ref[at, p * LANES : (p + 1) * LANES]
            swapped = pltpu.roll(both, BLOCK, 1)
            rows += [
                jnp.where(first, both, 0.0),
                jnp.where(first, 0.0, swapped),
                jnp.where(first, swapped, 0.0),
                jnp.where(first, 0.0, both),
            ]
        left = jnp.concatenate(rows, 0).astype(BF16)
        packed = [[], []]
        for half in range(2):
            out = dot(left, stacked(tile_ref, at, half), NT).astype(BF16)
            for s in range(2 * vecs):
                shift = half * 2 * vecs + s
                for v in range(2):
                    part = out[s * GROUP : (s + 1) * GROUP, v * LANES : (v + 1) * LANES]
                    packed[v].append((pltpu.roll(part, shift, 1) if shift else part) * masks[shift])
        for v in range(2):
            part = sum(packed[v][1:], packed[v][0]).astype(F32)
            part = pltpu.roll(part, LANES + 1 - GROUP, 1, stride=1, stride_axis=0)
            packed_ref[at, v * LANES : (v + 1) * LANES] = part.astype(BF16)
        return 0

    lax.fori_loop(0, x_ref.shape[0] // GROUP, step, 0, unroll=8)
    out_ref[...] = dot(packed_ref[...], order_ref[...], NT).astype(BF16)


def forward(vecs, bases, index, pieces, order, tile):
    slots, wide = tile.shape[0], vecs * BLOCK
    whole = pl.BlockSpec(memory_space=pltpu.VMEM)
    return pl.pallas_call(
        functools.partial(forward_kernel, vecs),
        out_shape=jax.ShapeDtypeStruct((slots, wide), BF16),
        in_specs=[pl.BlockSpec(memory_space=pltpu.SMEM)] + [whole] * (len(pieces) + 3),
        out_specs=whole,
        scratch_shapes=[
            pltpu.VMEM((slots, wide), F32),
            pltpu.VMEM((slots, wide), BF16),
        ],
        compiler_params=params(20),
        name="forward",
    )(bases, index, *pieces, order, tile)


def backward_kernel(vecs, y_ref, route_ref, tile_ref, out_ref, wide_ref):
    shape = (out_ref.shape[0], SIZE)
    own = (
        lax.broadcasted_iota(jnp.int32, shape, 1) % GROUP == lax.broadcasted_iota(jnp.int32, shape, 0) % GROUP
    )
    far = y_ref[...].astype(F32).T.astype(BF16)
    for s in range(2 * vecs):
        part = dot(far, route_ref[s * SIZE : (s + 1) * SIZE, :], NT)
        wide_ref[:, s * SIZE : (s + 1) * SIZE] = jnp.where(own, part, 0.0).astype(BF16)
    first = lax.broadcasted_iota(jnp.int32, (GROUP, LANES), 1) < BLOCK
    span = HALF * GROUP

    def step(g, _):
        at = pl.ds(pl.multiple_of(g * GROUP, GROUP), GROUP)
        out = None
        for half in range(2):
            left = [
                wide_ref[at, s * SIZE + half * span : s * SIZE + (half + 1) * span] for s in range(2 * vecs)
            ]
            part = dot(jnp.concatenate(left, 0), stacked(tile_ref, at, half))
            out = part if out is None else out + part
        sums = []
        for k in range(vecs):
            even, odd = out[2 * k * GROUP : (2 * k + 1) * GROUP], out[(2 * k + 1) * GROUP : (2 * k + 2) * GROUP]
            part = jnp.where(first, even, odd)
            sums.append(part + pltpu.roll(part, BLOCK, 1))
        for p in range(vecs // 2):
            out_ref[at, p * LANES : (p + 1) * LANES] = jnp.where(first, sums[2 * p], sums[2 * p + 1]).astype(BF16)
        return 0

    lax.fori_loop(0, out_ref.shape[0] // GROUP, step, 0, unroll=8)


def backward(vecs, far, route, tile):
    wide, slots = far.shape
    whole = pl.BlockSpec(memory_space=pltpu.VMEM)
    return pl.pallas_call(
        functools.partial(backward_kernel, vecs),
        out_shape=jax.ShapeDtypeStruct((slots, wide), BF16),
        in_specs=[whole] * 3,
        out_specs=whole,
        scratch_shapes=[
            pltpu.VMEM((slots, 2 * vecs * SIZE), BF16),
        ],
        compiler_params=params(20),
        name="backward",
    )(far, route, tile)


def spread_kernel(col_ref, row_ref, back_ref, forth_ref, out_ref):
    count = out_ref.shape[0]
    place = lax.broadcasted_iota(jnp.int32, (count, col_ref.shape[1]), 0) + pl.program_id(0) * count
    total = dot(as_ones(place == col_ref[...]), back_ref[...])
    total += dot(as_ones(place == row_ref[...]), forth_ref[...])
    out_ref[...] = total.astype(BF16)


def spread(col_index, row_index, back, forth, blocks):
    whole = pl.BlockSpec(memory_space=pltpu.VMEM)
    step = WIDTH
    return pl.pallas_call(
        spread_kernel,
        grid=(blocks // step,),
        out_shape=jax.ShapeDtypeStruct((blocks, back.shape[1]), BF16),
        in_specs=[whole] * 4,
        out_specs=pl.BlockSpec((step, back.shape[1]), lambda i: (i, 0)),
        compiler_params=params(20),
        name="spread",
    )(col_index, row_index, back, forth)


def body(x_vec, hx_vec, p_vec, hp_vec, theta, precond, tile_vals, tile_rows, tile_cols, tile_count):
    vecs, piece_len = x_vec.shape
    rows, cols = lax.axis_size("row"), lax.axis_size("col")
    ring = rows // 2
    ndim_total = piece_len * rows * cols
    row_pos = lax.axis_index("row")
    width = piece_len // BLOCK
    slots = tile_vals.shape[2]
    tile = tile_vals[0, 0]
    residue = (hx_vec - x_vec * theta[:, None]) / precond[None, :]
    live = jnp.arange(slots, dtype=jnp.int32) < tile_count[0, 0]
    row_index = jnp.where(live, tile_rows[0, 0], -1)[None]
    col_index = jnp.where(live, tile_cols[0, 0], -1)[None]

    def along(block, sign):
        path = [(r * cols + c, r * cols + (c + sign * r) % cols) for r in range(rows) for c in range(cols)]
        return lax.ppermute(block, BOTH, path)

    def within(block, flip, turn):
        return lax.ppermute(
            block, "row", [(i, (i // ring ^ flip) * ring + (i % ring + turn) % ring) for i in range(rows)]
        )

    own = residue.astype(BF16).reshape(vecs, width, BLOCK).transpose(0, 2, 1).reshape(vecs * BLOCK, width)
    across = within(own, 1, 0)
    pieces = [own, across] + [within(own, 0, n) for n in (1, 3, 2)]
    pieces += [within(across, 0, n) for n in (1, 3, 2)]
    flips = jnp.array([0, 1, 0, 0, 0, 1, 1, 1], jnp.int32)
    turns = jnp.array([0, 0, 1, 3, 2, 1, 3, 2], jnp.int32)
    bases = width * ((row_pos // ring ^ flips) * ring + (row_pos % ring - turns) % ring)
    far_index = along(lax.optimization_barrier((row_index, across))[0], 1)
    held = stage(lax.optimization_barrier((tile, pieces[2]))[0])
    picked, far_order = pick(bases, far_index, pieces)
    far = along(picked, -1)
    forth = along(forward(vecs, bases, col_index, pieces, order_matrix(vecs), held), 1)
    back = backward(vecs, far, route_matrix(vecs), held)
    parts = spread(col_index, far_order, back, forth, rows * width).reshape(rows, width, vecs * BLOCK)
    parts = lax.all_to_all(parts, "row", 0, 0, tiled=True)
    total = parts.astype(F32).sum(0)
    hw_vec = total.reshape(width, vecs, BLOCK).transpose(1, 0, 2).reshape(vecs, piece_len)

    vectors = jnp.concatenate([x_vec, residue, p_vec], 0)
    known = jnp.concatenate([vectors, hx_vec, hp_vec], 0)
    early = jnp.dot(vectors, known.T, precision=lax.Precision.HIGHEST, preferred_element_type=F32)
    late = jnp.dot(vectors, hw_vec.T, precision=lax.Precision.HIGHEST, preferred_element_type=F32)
    gram = jnp.concatenate([early, late], 1)
    flat = jnp.pad(gram.reshape(-1), (0, 3 * LANES - gram.size)).reshape(1, 3, LANES)
    flat = jnp.broadcast_to(flat, (rows * cols, 3, LANES))
    gram = lax.all_to_all(flat, BOTH, 0, 0, tiled=True).sum(0).reshape(-1)[: gram.size].reshape(gram.shape)
    gram = gram / ndim_total
    n = 3 * vecs
    gram_a = jnp.concatenate([gram[:, n : n + vecs], gram[:, n + 2 * vecs :], gram[:, n + vecs : n + 2 * vecs]], 1)
    return hw_vec, gram_a, gram[:, :n]


def solution(mesh):
    vector = P(None, ("col", "row"))
    placed = (
        vector,
        vector,
        vector,
        vector,
        P(),
        P(("col", "row")),
        P("row", "col", None, None),
        P("row", "col", None),
        P("row", "col", None),
        P("row", "col"),
    )
    return jax.shard_map(body, mesh=mesh, in_specs=placed, out_specs=(vector, P(), P()), check_vma=False)
```

```python
import functools

import jax
import jax.numpy as jnp
import numpy as np
from jax import lax
from jax.experimental import pallas as pl
from jax.experimental.pallas import tpu as pltpu
from jax.sharding import PartitionSpec as P

BLOCK = 64
LANES = 128
PAIRS = BLOCK * BLOCK // LANES
GROUP = 16
HALF = PAIRS // 2
SIZE = PAIRS * GROUP
WIDTH = 1024
BOTH = ("row", "col")
NT = (((1,), (1,)), ((), ()))
NN = (((1,), (0,)), ((), ()))
F32 = jnp.float32
BF16 = jnp.bfloat16


def params(mib):
    return pltpu.CompilerParams(vmem_limit_bytes=mib << 20)


def dot(a, b, dims=NN):
    return lax.dot_general(a, b, dims, preferred_element_type=F32)


def as_ones(mask):
    return jnp.where(mask, 1.0, 0.0).astype(BF16)


def gathered(base_ref, index, piece_refs):
    shape = (piece_refs[0].shape[1], index.shape[1])
    place = index - lax.broadcasted_iota(jnp.int32, shape, 0)
    total = None
    for d, piece in enumerate(piece_refs):
        part = dot(piece[...], as_ones(place == base_ref[d]))
        total = part if total is None else total + part
    return total


def masked(index, count):
    return jnp.where(lax.broadcasted_iota(jnp.int32, index.shape, 1) < count, index, -1)


def pick_kernel(base_ref, index_ref, *refs):
    pieces, (out_ref, turned_ref) = refs[:-2], refs[-2:]
    turned_ref[...] = turned_slots(index_ref[...])
    out_ref[...] = gathered(base_ref, index_ref[...], pieces).astype(BF16)


def pick(bases, index, pieces):
    whole = pl.BlockSpec(memory_space=pltpu.VMEM)
    return pl.pallas_call(
        pick_kernel,
        out_shape=(
            jax.ShapeDtypeStruct((pieces[0].shape[0], index.shape[1]), BF16),
            jax.ShapeDtypeStruct(index.shape, index.dtype),
        ),
        in_specs=[pl.BlockSpec(memory_space=pltpu.SMEM)] + [whole] * (1 + len(pieces)),
        out_specs=(whole, whole),
        compiler_params=params(16),
        name="pick",
    )(bases, index, *pieces)


def order_matrix(vecs):
    place = np.arange(vecs * BLOCK)
    pair, kind = place // GROUP, place % GROUP
    half, k, parity = kind // (2 * vecs), kind % (2 * vecs) // 2, kind % 2
    entry = k * BLOCK + 2 * (half * HALF + pair) + parity
    return jnp.asarray(np.arange(vecs * BLOCK)[:, None] == entry, BF16)


def route_matrix(vecs):
    row = np.arange(2 * vecs * SIZE)[:, None]
    kind, pair = row // SIZE, row % SIZE // GROUP
    return jnp.asarray(np.arange(vecs * BLOCK) == kind // 2 * BLOCK + 2 * pair + kind % 2, BF16)


def turned_slots(index):
    lane = lax.broadcasted_iota(jnp.int32, (1, LANES), 1)
    parts = []
    for n in range(index.shape[1] // LANES):
        part = index[:, n * LANES : (n + 1) * LANES]
        for bit in (1, 2, 4, 8):
            part = jnp.where(lane & bit != 0, pltpu.roll(part, bit, 1), pltpu.roll(part, LANES - bit, 1))
        parts.append(part)
    return jnp.concatenate(parts, 1)


def stage_kernel(tile_ref, out_ref, sem):
    copy = pltpu.make_async_copy(tile_ref, out_ref, sem)
    copy.start()
    copy.wait()


def stage(tile):
    return pl.pallas_call(
        stage_kernel,
        out_shape=jax.ShapeDtypeStruct(tile.shape, tile.dtype),
        in_specs=[pl.BlockSpec(memory_space=pl.ANY)],
        out_specs=pl.BlockSpec(memory_space=pltpu.VMEM),
        scratch_shapes=[pltpu.SemaphoreType.DMA],
        compiler_params=params(12),
        name="stage",
    )(tile)


def stacked(tile_ref, at, half):
    parts = [tile_ref[at, c * LANES : (c + 1) * LANES] for c in range(half * HALF, (half + 1) * HALF)]
    return jnp.concatenate(parts, 0)


def forward_kernel(vecs, base_ref, count_ref, index_ref, *refs):
    pieces, (order_ref, tile_ref, out_ref, x_ref, packed_ref) = refs[:-5], refs[-5:]
    x_ref[...] = gathered(base_ref, turned_slots(masked(index_ref[...], count_ref[0])), pieces).T
    lane = lax.broadcasted_iota(jnp.int32, (GROUP, LANES), 1)
    row = lax.broadcasted_iota(jnp.int32, (GROUP, LANES), 0)
    first = lane < BLOCK
    masks = [as_ones((lane + row + 1) % GROUP == n) for n in range(GROUP)]

    def step(g, _):
        at = pl.ds(pl.multiple_of(g * GROUP, GROUP), GROUP)
        rows = []
        for p in range(vecs // 2):
            both = x_ref[at, p * LANES : (p + 1) * LANES]
            swapped = pltpu.roll(both, BLOCK, 1)
            rows += [
                jnp.where(first, both, 0.0),
                jnp.where(first, 0.0, swapped),
                jnp.where(first, swapped, 0.0),
                jnp.where(first, 0.0, both),
            ]
        left = jnp.concatenate(rows, 0).astype(BF16)
        packed = [[], []]
        for half in range(2):
            out = dot(left, stacked(tile_ref, at, half), NT).astype(BF16)
            for s in range(2 * vecs):
                shift = half * 2 * vecs + s
                for v in range(2):
                    part = out[s * GROUP : (s + 1) * GROUP, v * LANES : (v + 1) * LANES]
                    packed[v].append((pltpu.roll(part, shift, 1) if shift else part) * masks[shift])
        for v in range(2):
            part = sum(packed[v][1:], packed[v][0]).astype(F32)
            part = pltpu.roll(part, LANES + 1 - GROUP, 1, stride=1, stride_axis=0)
            packed_ref[at, v * LANES : (v + 1) * LANES] = part.astype(BF16)
        return 0

    lax.fori_loop(0, x_ref.shape[0] // GROUP, step, 0, unroll=8)
    out_ref[...] = dot(packed_ref[...], order_ref[...], NT).astype(BF16)


def forward(vecs, bases, used, index, pieces, order, tile):
    slots, wide = tile.shape[0], vecs * BLOCK
    whole = pl.BlockSpec(memory_space=pltpu.VMEM)
    return pl.pallas_call(
        functools.partial(forward_kernel, vecs),
        out_shape=jax.ShapeDtypeStruct((slots, wide), BF16),
        in_specs=[pl.BlockSpec(memory_space=pltpu.SMEM)] * 2 + [whole] * (len(pieces) + 3),
        out_specs=whole,
        scratch_shapes=[
            pltpu.VMEM((slots, wide), F32),
            pltpu.VMEM((slots, wide), BF16),
        ],
        compiler_params=params(20),
        name="forward",
    )(bases, used, index, *pieces, order, tile)


def backward_kernel(vecs, y_ref, route_ref, tile_ref, out_ref, wide_ref):
    shape = (out_ref.shape[0], SIZE)
    own = (
        lax.broadcasted_iota(jnp.int32, shape, 1) % GROUP == lax.broadcasted_iota(jnp.int32, shape, 0) % GROUP
    )
    far = y_ref[...].astype(F32).T.astype(BF16)
    for s in range(2 * vecs):
        part = dot(far, route_ref[s * SIZE : (s + 1) * SIZE, :], NT)
        wide_ref[:, s * SIZE : (s + 1) * SIZE] = jnp.where(own, part, 0.0).astype(BF16)
    first = lax.broadcasted_iota(jnp.int32, (GROUP, LANES), 1) < BLOCK
    span = HALF * GROUP

    def step(g, _):
        at = pl.ds(pl.multiple_of(g * GROUP, GROUP), GROUP)
        out = None
        for half in range(2):
            left = [
                wide_ref[at, s * SIZE + half * span : s * SIZE + (half + 1) * span] for s in range(2 * vecs)
            ]
            part = dot(jnp.concatenate(left, 0), stacked(tile_ref, at, half))
            out = part if out is None else out + part
        sums = []
        for k in range(vecs):
            even, odd = out[2 * k * GROUP : (2 * k + 1) * GROUP], out[(2 * k + 1) * GROUP : (2 * k + 2) * GROUP]
            part = jnp.where(first, even, odd)
            sums.append(part + pltpu.roll(part, BLOCK, 1))
        for p in range(vecs // 2):
            out_ref[at, p * LANES : (p + 1) * LANES] = jnp.where(first, sums[2 * p], sums[2 * p + 1]).astype(BF16)
        return 0

    lax.fori_loop(0, out_ref.shape[0] // GROUP, step, 0, unroll=8)


def backward(vecs, far, route, tile):
    wide, slots = far.shape
    whole = pl.BlockSpec(memory_space=pltpu.VMEM)
    return pl.pallas_call(
        functools.partial(backward_kernel, vecs),
        out_shape=jax.ShapeDtypeStruct((slots, wide), BF16),
        in_specs=[whole] * 3,
        out_specs=whole,
        scratch_shapes=[
            pltpu.VMEM((slots, 2 * vecs * SIZE), BF16),
        ],
        compiler_params=params(20),
        name="backward",
    )(far, route, tile)


def spread_kernel(count_ref, col_ref, row_ref, back_ref, forth_ref, out_ref):
    count = out_ref.shape[0]
    place = lax.broadcasted_iota(jnp.int32, (count, col_ref.shape[1]), 0) + pl.program_id(0) * count
    total = dot(as_ones(place == masked(col_ref[...], count_ref[0])), back_ref[...])
    total += dot(as_ones(place == row_ref[...]), forth_ref[...])
    out_ref[...] = total.astype(BF16)


def spread(used, col_index, row_index, back, forth, blocks):
    whole = pl.BlockSpec(memory_space=pltpu.VMEM)
    step = WIDTH
    return pl.pallas_call(
        spread_kernel,
        grid=(blocks // step,),
        out_shape=jax.ShapeDtypeStruct((blocks, back.shape[1]), BF16),
        in_specs=[pl.BlockSpec(memory_space=pltpu.SMEM)] + [whole] * 4,
        out_specs=pl.BlockSpec((step, back.shape[1]), lambda i: (i, 0)),
        compiler_params=params(20),
        name="spread",
    )(used, col_index, row_index, back, forth)


def total_kernel(vecs, part_ref, vector_ref, early_ref, sum_ref, gram_ref):
    total = part_ref[0].astype(F32)
    for n in range(1, part_ref.shape[0]):
        total += part_ref[n].astype(F32)
    sum_ref[...] = total
    lines = []
    for p in range(3 * vecs // 2):
        pair = vector_ref[:, p * LANES : (p + 1) * LANES]
        swapped = pltpu.roll(pair, BLOCK, 1)
        for q in range(vecs // 2):
            both = total[:, q * LANES : (q + 1) * LANES]
            lines += [(pair * both).sum(0, keepdims=True), (swapped * both).sum(0, keepdims=True)]
    lines = jnp.concatenate(lines, 0)
    shape = lines.shape
    row = lax.broadcasted_iota(jnp.int32, shape, 0)
    lane = lax.broadcasted_iota(jnp.int32, shape, 1)
    swap, q, p = row % 2, row // 2 % (vecs // 2), row // vecs
    even = (2 * p + swap) * vecs + 2 * q
    odd = (2 * p + 1 - swap) * vecs + 2 * q + 1
    late = jnp.where(lane == even, lines[:, :BLOCK].sum(1, keepdims=True), 0.0)
    late += jnp.where(lane == odd, lines[:, BLOCK:].sum(1, keepdims=True), 0.0)
    packed = jnp.concatenate([early_ref[...], late.sum(0, keepdims=True)], 0)
    gram_ref[...] = jnp.broadcast_to(packed[None], gram_ref.shape)


def totalled(vecs, parts, vectors, early, peers):
    whole = pl.BlockSpec(memory_space=pltpu.VMEM)
    return pl.pallas_call(
        functools.partial(total_kernel, vecs),
        out_shape=(
            jax.ShapeDtypeStruct(parts.shape[1:], F32),
            jax.ShapeDtypeStruct((peers, early.shape[0] + 1, LANES), F32),
        ),
        in_specs=[whole] * 3,
        out_specs=(whole, whole),
        compiler_params=params(12),
        name="totalled",
    )(parts, vectors, early)


def unpack_kernel(vecs, scale, gram_ref, a_ref, b_ref):
    packed = gram_ref[0]
    for n in range(1, gram_ref.shape[0]):
        packed += gram_ref[n]
    packed = packed * scale
    wide, half = 5 * vecs, 3 * vecs // 2
    lane = lax.broadcasted_iota(jnp.int32, (1, LANES), 1)

    def shifted(line, by):
        by = by % LANES
        return pltpu.roll(packed[line : line + 1], by, 1) if by else packed[line : line + 1]

    for m in range(3 * vecs):
        line, at = m // half, m % half * wide
        b_ref[m : m + 1, :] = shifted(line, -at)[:, : 3 * vecs]
        first, last = shifted(line, -at - 3 * vecs), shifted(line, -at - 2 * vecs)
        middle = shifted(2, vecs - m * vecs)
        mixed = jnp.where(lane < vecs, first, jnp.where(lane < 2 * vecs, middle, last))
        a_ref[m : m + 1, :] = mixed[:, : 3 * vecs]


def unpacked(vecs, gram, scale):
    whole = pl.BlockSpec(memory_space=pltpu.VMEM)
    shape = jax.ShapeDtypeStruct((3 * vecs, 3 * vecs), F32)
    return pl.pallas_call(
        functools.partial(unpack_kernel, vecs, scale),
        out_shape=(shape, shape),
        in_specs=[whole],
        out_specs=(whole, whole),
        compiler_params=params(12),
        name="unpacked",
    )(gram)


def body(x_vec, hx_vec, p_vec, hp_vec, theta, precond, tile_vals, tile_rows, tile_cols, tile_count):
    vecs, piece_len = x_vec.shape
    rows, cols = lax.axis_size("row"), lax.axis_size("col")
    ring = rows // 2
    ndim_total = piece_len * rows * cols
    row_pos = lax.axis_index("row")
    width = piece_len // BLOCK
    slots = tile_vals.shape[2]
    tile = tile_vals[0, 0]
    residue = (hx_vec - x_vec * theta[:, None]) / precond[None, :]
    live = jnp.arange(slots, dtype=jnp.int32) < tile_count[0, 0]
    row_index = jnp.where(live, tile_rows[0, 0], -1)[None]
    col_index = tile_cols[0, 0][None]
    used = tile_count.reshape(1)

    def along(block, sign):
        path = [(r * cols + c, r * cols + (c + sign * r) % cols) for r in range(rows) for c in range(cols)]
        return lax.ppermute(block, BOTH, path)

    def within(block, flip, turn):
        return lax.ppermute(
            block, "row", [(i, (i // ring ^ flip) * ring + (i % ring + turn) % ring) for i in range(rows)]
        )

    own = residue.astype(BF16).reshape(vecs, width, BLOCK).transpose(0, 2, 1).reshape(vecs * BLOCK, width)
    across = within(own, 1, 0)
    pieces = [own, across] + [within(own, 0, n) for n in (1, 3, 2)]
    pieces += [within(across, 0, n) for n in (1, 3, 2)]
    flips = jnp.array([0, 1, 0, 0, 0, 1, 1, 1], jnp.int32)
    turns = jnp.array([0, 0, 1, 3, 2, 1, 3, 2], jnp.int32)
    bases = width * ((row_pos // ring ^ flips) * ring + (row_pos % ring - turns) % ring)
    far_index = along(lax.optimization_barrier((row_index, pieces[2]))[0], 1)
    held = stage(lax.optimization_barrier((tile, pieces[2]))[0])
    picked, far_order = pick(bases, far_index, pieces)
    far = along(picked, -1)
    forth = along(forward(vecs, bases, used, col_index, pieces, order_matrix(vecs), held), 1)
    back = backward(vecs, far, route_matrix(vecs), held)
    parts = spread(used, col_index, far_order, back, forth, rows * width).reshape(rows, width, vecs * BLOCK)
    parts = lax.all_to_all(parts, "row", 0, 0, tiled=True)
    vectors = jnp.concatenate([x_vec, residue, p_vec], 0)
    known = jnp.concatenate([vectors, hx_vec, hp_vec], 0)
    early = jnp.dot(vectors, known.T, precision=lax.Precision.HIGHEST, preferred_element_type=F32)
    early = early.reshape(2, -1)
    early = jnp.pad(early, ((0, 0), (0, LANES - early.shape[1])))
    blocked = vectors.reshape(-1, width, BLOCK).transpose(1, 0, 2).reshape(width, -1)
    total, gram = totalled(vecs, parts, blocked, early, rows * cols)
    hw_vec = total.reshape(width, vecs, BLOCK).transpose(1, 0, 2).reshape(vecs, piece_len)
    gram = lax.all_to_all(gram, BOTH, 0, 0, tiled=True)
    gram_a, gram_b = unpacked(vecs, gram, 1.0 / ndim_total)
    return hw_vec, gram_a, gram_b


def solution(mesh):
    vector = P(None, ("col", "row"))
    placed = (
        vector,
        vector,
        vector,
        vector,
        P(),
        P(("col", "row")),
        P("row", "col", None, None),
        P("row", "col", None),
        P("row", "col", None),
        P("row", "col"),
    )
    return jax.shard_map(body, mesh=mesh, in_specs=placed, out_specs=(vector, P(), P()), check_vma=False)
```

```python
import functools

import jax
import jax.numpy as jnp
import numpy as np
from jax import lax
from jax.experimental import pallas as pl
from jax.experimental.pallas import tpu as pltpu
from jax.sharding import PartitionSpec as P

BLOCK = 64
LANES = 128
PAIRS = BLOCK * BLOCK // LANES
GROUP = 16
HALF = PAIRS // 2
SIZE = PAIRS * GROUP
WIDTH = 1024
BOTH = ("row", "col")
NT = (((1,), (1,)), ((), ()))
NN = (((1,), (0,)), ((), ()))
F32 = jnp.float32
BF16 = jnp.bfloat16


def params(mib):
    return pltpu.CompilerParams(vmem_limit_bytes=mib << 20)


def dot(a, b, dims=NN):
    return lax.dot_general(a, b, dims, preferred_element_type=F32)


def as_ones(mask):
    return jnp.where(mask, 1.0, 0.0).astype(BF16)


def gathered(base_ref, index, piece_refs):
    shape = (piece_refs[0].shape[1], index.shape[1])
    place = index - lax.broadcasted_iota(jnp.int32, shape, 0)
    total = None
    for d, piece in enumerate(piece_refs):
        part = dot(piece[...], as_ones(place == base_ref[d]))
        total = part if total is None else total + part
    return total


def masked(index, count):
    return jnp.where(lax.broadcasted_iota(jnp.int32, index.shape, 1) < count, index, -1)


def early_kernel(base_ref, count_ref, far_ref, own_ref, *refs):
    pieces, (tile_ref, picked_ref, x_ref, far_order_ref, held_ref, sem) = refs[:-6], refs[-6:]
    copy = pltpu.make_async_copy(tile_ref, held_ref, sem)
    copy.start()
    far_order_ref[...] = turned_slots(far_ref[...])
    picked_ref[...] = gathered(base_ref, far_ref[...], pieces).astype(BF16)
    own_order = turned_slots(masked(own_ref[...], count_ref[0]))
    x_ref[...] = gathered(base_ref, own_order, pieces).astype(BF16)
    copy.wait()


def early_pick(bases, used, far_index, own_index, pieces, tile):
    whole = pl.BlockSpec(memory_space=pltpu.VMEM)
    shape = jax.ShapeDtypeStruct((pieces[0].shape[0], far_index.shape[1]), BF16)
    return pl.pallas_call(
        early_kernel,
        out_shape=(
            shape,
            shape,
            jax.ShapeDtypeStruct(far_index.shape, far_index.dtype),
            jax.ShapeDtypeStruct(tile.shape, tile.dtype),
        ),
        in_specs=[pl.BlockSpec(memory_space=pltpu.SMEM)] * 2
        + [whole] * (2 + len(pieces))
        + [pl.BlockSpec(memory_space=pl.ANY)],
        out_specs=(whole,) * 4,
        scratch_shapes=[pltpu.SemaphoreType.DMA],
        compiler_params=params(42),
        name="early_pick",
    )(bases, used, far_index, own_index, *pieces, tile)


def pick_kernel(base_ref, index_ref, before_ref, *refs):
    total = gathered(base_ref, index_ref[...], refs[:-1])
    refs[-1][...] = (before_ref[...].astype(F32) + total).astype(BF16)


def pick(bases, index, before, pieces):
    whole = pl.BlockSpec(memory_space=pltpu.VMEM)
    return pl.pallas_call(
        pick_kernel,
        out_shape=jax.ShapeDtypeStruct(before.shape, BF16),
        in_specs=[pl.BlockSpec(memory_space=pltpu.SMEM)] + [whole] * (2 + len(pieces)),
        out_specs=whole,
        compiler_params=params(16),
        name="pick",
    )(bases, index, before, *pieces)


def order_matrix(vecs):
    place = np.arange(vecs * BLOCK)
    pair, kind = place // GROUP, place % GROUP
    half, k, parity = kind // (2 * vecs), kind % (2 * vecs) // 2, kind % 2
    entry = k * BLOCK + 2 * (half * HALF + pair) + parity
    return jnp.asarray(np.arange(vecs * BLOCK)[:, None] == entry, BF16)


def route_matrix(vecs):
    row = np.arange(2 * vecs * SIZE)[:, None]
    kind, pair = row // SIZE, row % SIZE // GROUP
    return jnp.asarray(np.arange(vecs * BLOCK) == kind // 2 * BLOCK + 2 * pair + kind % 2, BF16)


def turned_slots(index):
    lane = lax.broadcasted_iota(jnp.int32, (1, LANES), 1)
    parts = []
    for n in range(index.shape[1] // LANES):
        part = index[:, n * LANES : (n + 1) * LANES]
        for bit in (1, 2, 4, 8):
            part = jnp.where(lane & bit != 0, pltpu.roll(part, bit, 1), pltpu.roll(part, LANES - bit, 1))
        parts.append(part)
    return jnp.concatenate(parts, 1)


def stacked(tile_ref, at, half):
    parts = [tile_ref[at, c * LANES : (c + 1) * LANES] for c in range(half * HALF, (half + 1) * HALF)]
    return jnp.concatenate(parts, 0)


def forward_kernel(vecs, base_ref, count_ref, index_ref, before_ref, *refs):
    pieces, (order_ref, tile_ref, out_ref, x_ref, packed_ref) = refs[:-5], refs[-5:]
    own_order = turned_slots(masked(index_ref[...], count_ref[0]))
    x_ref[...] = (before_ref[...].astype(F32) + gathered(base_ref, own_order, pieces)).T
    lane = lax.broadcasted_iota(jnp.int32, (GROUP, LANES), 1)
    row = lax.broadcasted_iota(jnp.int32, (GROUP, LANES), 0)
    first = lane < BLOCK
    masks = [as_ones((lane + row + 1) % GROUP == n) for n in range(GROUP)]

    def step(g, _):
        at = pl.ds(pl.multiple_of(g * GROUP, GROUP), GROUP)
        rows = []
        for p in range(vecs // 2):
            both = x_ref[at, p * LANES : (p + 1) * LANES]
            swapped = pltpu.roll(both, BLOCK, 1)
            rows += [
                jnp.where(first, both, 0.0),
                jnp.where(first, 0.0, swapped),
                jnp.where(first, swapped, 0.0),
                jnp.where(first, 0.0, both),
            ]
        left = jnp.concatenate(rows, 0).astype(BF16)
        packed = [[], []]
        for half in range(2):
            out = dot(left, stacked(tile_ref, at, half), NT).astype(BF16)
            for s in range(2 * vecs):
                shift = half * 2 * vecs + s
                for v in range(2):
                    part = out[s * GROUP : (s + 1) * GROUP, v * LANES : (v + 1) * LANES]
                    packed[v].append((pltpu.roll(part, shift, 1) if shift else part) * masks[shift])
        for v in range(2):
            part = sum(packed[v][1:], packed[v][0]).astype(F32)
            part = pltpu.roll(part, LANES + 1 - GROUP, 1, stride=1, stride_axis=0)
            packed_ref[at, v * LANES : (v + 1) * LANES] = part.astype(BF16)
        return 0

    lax.fori_loop(0, x_ref.shape[0] // GROUP, step, 0, unroll=8)
    out_ref[...] = dot(packed_ref[...], order_ref[...], NT).astype(BF16)


def forward(vecs, bases, used, index, before, pieces, order, tile):
    slots, wide = tile.shape[0], vecs * BLOCK
    whole = pl.BlockSpec(memory_space=pltpu.VMEM)
    return pl.pallas_call(
        functools.partial(forward_kernel, vecs),
        out_shape=jax.ShapeDtypeStruct((slots, wide), BF16),
        in_specs=[pl.BlockSpec(memory_space=pltpu.SMEM)] * 2 + [whole] * (len(pieces) + 4),
        out_specs=whole,
        scratch_shapes=[
            pltpu.VMEM((slots, wide), F32),
            pltpu.VMEM((slots, wide), BF16),
        ],
        compiler_params=params(20),
        name="forward",
    )(bases, used, index, before, *pieces, order, tile)


def backward_kernel(vecs, y_ref, route_ref, tile_ref, out_ref, wide_ref):
    shape = (out_ref.shape[0], SIZE)
    own = (
        lax.broadcasted_iota(jnp.int32, shape, 1) % GROUP == lax.broadcasted_iota(jnp.int32, shape, 0) % GROUP
    )
    far = y_ref[...].astype(F32).T.astype(BF16)
    for s in range(2 * vecs):
        part = dot(far, route_ref[s * SIZE : (s + 1) * SIZE, :], NT)
        wide_ref[:, s * SIZE : (s + 1) * SIZE] = jnp.where(own, part, 0.0).astype(BF16)
    first = lax.broadcasted_iota(jnp.int32, (GROUP, LANES), 1) < BLOCK
    span = HALF * GROUP

    def step(g, _):
        at = pl.ds(pl.multiple_of(g * GROUP, GROUP), GROUP)
        out = None
        for half in range(2):
            left = [
                wide_ref[at, s * SIZE + half * span : s * SIZE + (half + 1) * span] for s in range(2 * vecs)
            ]
            part = dot(jnp.concatenate(left, 0), stacked(tile_ref, at, half))
            out = part if out is None else out + part
        sums = []
        for k in range(vecs):
            even, odd = out[2 * k * GROUP : (2 * k + 1) * GROUP], out[(2 * k + 1) * GROUP : (2 * k + 2) * GROUP]
            part = jnp.where(first, even, odd)
            sums.append(part + pltpu.roll(part, BLOCK, 1))
        for p in range(vecs // 2):
            out_ref[at, p * LANES : (p + 1) * LANES] = jnp.where(first, sums[2 * p], sums[2 * p + 1]).astype(BF16)
        return 0

    lax.fori_loop(0, out_ref.shape[0] // GROUP, step, 0, unroll=8)


def backward(vecs, far, route, tile):
    wide, slots = far.shape
    whole = pl.BlockSpec(memory_space=pltpu.VMEM)
    return pl.pallas_call(
        functools.partial(backward_kernel, vecs),
        out_shape=jax.ShapeDtypeStruct((slots, wide), BF16),
        in_specs=[whole] * 3,
        out_specs=whole,
        scratch_shapes=[
            pltpu.VMEM((slots, 2 * vecs * SIZE), BF16),
        ],
        compiler_params=params(20),
        name="backward",
    )(far, route, tile)


def spread_kernel(count_ref, index_ref, part_ref, *refs):
    before, out_ref = refs[:-1], refs[-1]
    count = out_ref.shape[0]
    base = pl.program_id(0) * count
    place = lax.broadcasted_iota(jnp.int32, (count, index_ref.shape[1]), 0) + base
    total = dot(as_ones(place == masked(index_ref[...], count_ref[0])), part_ref[...])
    for more in before:
        total += more[pl.ds(pl.multiple_of(base, count), count), :]
    out_ref[...] = total.astype(out_ref.dtype)


def spread(used, index, part, blocks, dtype, *before):
    whole = pl.BlockSpec(memory_space=pltpu.VMEM)
    return pl.pallas_call(
        spread_kernel,
        grid=(blocks // WIDTH,),
        out_shape=jax.ShapeDtypeStruct((blocks, part.shape[1]), dtype),
        in_specs=[pl.BlockSpec(memory_space=pltpu.SMEM)] + [whole] * (2 + len(before)),
        out_specs=pl.BlockSpec((WIDTH, part.shape[1]), lambda i: (i, 0)),
        compiler_params=params(20),
        name="spread",
    )(used, index, part, *before)


def total_kernel(vecs, part_ref, vector_ref, early_ref, sum_ref, gram_ref):
    total = part_ref[0].astype(F32)
    for n in range(1, part_ref.shape[0]):
        total += part_ref[n].astype(F32)
    sum_ref[...] = total
    lines = []
    for p in range(3 * vecs // 2):
        pair = vector_ref[:, p * LANES : (p + 1) * LANES]
        swapped = pltpu.roll(pair, BLOCK, 1)
        for q in range(vecs // 2):
            both = total[:, q * LANES : (q + 1) * LANES]
            lines += [(pair * both).sum(0, keepdims=True), (swapped * both).sum(0, keepdims=True)]
    lines = jnp.concatenate(lines, 0)
    shape = lines.shape
    row = lax.broadcasted_iota(jnp.int32, shape, 0)
    lane = lax.broadcasted_iota(jnp.int32, shape, 1)
    swap, q, p = row % 2, row // 2 % (vecs // 2), row // vecs
    even = (2 * p + swap) * vecs + 2 * q
    odd = (2 * p + 1 - swap) * vecs + 2 * q + 1
    late = jnp.where(lane == even, lines[:, :BLOCK].sum(1, keepdims=True), 0.0)
    late += jnp.where(lane == odd, lines[:, BLOCK:].sum(1, keepdims=True), 0.0)
    packed = jnp.concatenate([early_ref[...], late.sum(0, keepdims=True)], 0)
    gram_ref[...] = jnp.broadcast_to(packed[None], gram_ref.shape)


def totalled(vecs, parts, vectors, early, peers):
    whole = pl.BlockSpec(memory_space=pltpu.VMEM)
    return pl.pallas_call(
        functools.partial(total_kernel, vecs),
        out_shape=(
            jax.ShapeDtypeStruct(parts.shape[1:], F32),
            jax.ShapeDtypeStruct((peers, early.shape[0] + 1, LANES), F32),
        ),
        in_specs=[whole] * 3,
        out_specs=(whole, whole),
        compiler_params=params(12),
        name="totalled",
    )(parts, vectors, early)


def unpack_kernel(vecs, scale, gram_ref, a_ref, b_ref):
    packed = gram_ref[0]
    for n in range(1, gram_ref.shape[0]):
        packed += gram_ref[n]
    packed = packed * scale
    wide, half = 5 * vecs, 3 * vecs // 2
    lane = lax.broadcasted_iota(jnp.int32, (1, LANES), 1)

    def shifted(line, by):
        by = by % LANES
        return pltpu.roll(packed[line : line + 1], by, 1) if by else packed[line : line + 1]

    for m in range(3 * vecs):
        line, at = m // half, m % half * wide
        b_ref[m : m + 1, :] = shifted(line, -at)[:, : 3 * vecs]
        first, last = shifted(line, -at - 3 * vecs), shifted(line, -at - 2 * vecs)
        middle = shifted(2, vecs - m * vecs)
        mixed = jnp.where(lane < vecs, first, jnp.where(lane < 2 * vecs, middle, last))
        a_ref[m : m + 1, :] = mixed[:, : 3 * vecs]


def unpacked(vecs, gram, scale):
    whole = pl.BlockSpec(memory_space=pltpu.VMEM)
    shape = jax.ShapeDtypeStruct((3 * vecs, 3 * vecs), F32)
    return pl.pallas_call(
        functools.partial(unpack_kernel, vecs, scale),
        out_shape=(shape, shape),
        in_specs=[whole],
        out_specs=(whole, whole),
        compiler_params=params(12),
        name="unpacked",
    )(gram)


def body(x_vec, hx_vec, p_vec, hp_vec, theta, precond, tile_vals, tile_rows, tile_cols, tile_count):
    vecs, piece_len = x_vec.shape
    rows, cols = lax.axis_size("row"), lax.axis_size("col")
    ring = rows // 2
    ndim_total = piece_len * rows * cols
    row_pos = lax.axis_index("row")
    width = piece_len // BLOCK
    slots = tile_vals.shape[2]
    tile = tile_vals[0, 0]
    residue = (hx_vec - x_vec * theta[:, None]) / precond[None, :]
    live = jnp.arange(slots, dtype=jnp.int32) < tile_count[0, 0]
    row_index = jnp.where(live, tile_rows[0, 0], -1)[None]
    col_index = tile_cols[0, 0][None]
    used = tile_count.reshape(1)

    def along(block, sign):
        path = [(r * cols + c, r * cols + (c + sign * r) % cols) for r in range(rows) for c in range(cols)]
        return lax.ppermute(block, BOTH, path)

    def within(block, flip, turn):
        return lax.ppermute(
            block, "row", [(i, (i // ring ^ flip) * ring + (i % ring + turn) % ring) for i in range(rows)]
        )

    own = residue.astype(BF16).reshape(vecs, width, BLOCK).transpose(0, 2, 1).reshape(vecs * BLOCK, width)
    across = within(own, 1, 0)
    pieces = [own, across] + [within(own, 0, n) for n in (1, 3, 2)]
    pieces += [within(across, 0, n) for n in (1, 3, 2)]
    flips = jnp.array([0, 1, 0, 0, 0, 1, 1, 1], jnp.int32)
    turns = jnp.array([0, 0, 1, 3, 2, 1, 3, 2], jnp.int32)
    bases = width * ((row_pos // ring ^ flips) * ring + (row_pos % ring - turns) % ring)
    far_index = along(lax.optimization_barrier((row_index, pieces[2]))[0], 1)
    near = 5
    picked, x_slots, far_order, held = early_pick(
        bases[:near], used, far_index, col_index, pieces[:near], tile
    )
    far = along(pick(bases[near:], far_index, picked, pieces[near:]), -1)
    forth = forward(vecs, bases[near:], used, col_index, x_slots, pieces[near:], order_matrix(vecs), held)
    forth = along(forth, 1)
    back = backward(vecs, far, route_matrix(vecs), held)
    back = spread(used, col_index, back, rows * width, F32)
    every = jnp.full((1,), slots, jnp.int32)
    parts = spread(every, far_order, forth, rows * width, BF16, back).reshape(rows, width, vecs * BLOCK)
    parts = lax.all_to_all(parts, "row", 0, 0, tiled=True)
    vectors = jnp.concatenate([x_vec, residue, p_vec], 0)
    known = jnp.concatenate([vectors, hx_vec, hp_vec], 0)
    early = jnp.dot(vectors, known.T, precision=lax.Precision.HIGHEST, preferred_element_type=F32)
    early = early.reshape(2, -1)
    early = jnp.pad(early, ((0, 0), (0, LANES - early.shape[1])))
    blocked = vectors.reshape(-1, width, BLOCK).transpose(1, 0, 2).reshape(width, -1)
    total, gram = totalled(vecs, parts, blocked, early, rows * cols)
    hw_vec = total.reshape(width, vecs, BLOCK).transpose(1, 0, 2).reshape(vecs, piece_len)
    gram = lax.all_to_all(gram, BOTH, 0, 0, tiled=True)
    gram_a, gram_b = unpacked(vecs, gram, 1.0 / ndim_total)
    return hw_vec, gram_a, gram_b


def solution(mesh):
    vector = P(None, ("col", "row"))
    placed = (
        vector,
        vector,
        vector,
        vector,
        P(),
        P(("col", "row")),
        P("row", "col", None, None),
        P("row", "col", None),
        P("row", "col", None),
        P("row", "col"),
    )
    return jax.shard_map(body, mesh=mesh, in_specs=placed, out_specs=(vector, P(), P()), check_vma=False)
```

```python
import functools

import jax
import jax.numpy as jnp
import numpy as np
from jax import lax
from jax.experimental import pallas as pl
from jax.experimental.pallas import tpu as pltpu
from jax.sharding import PartitionSpec as P

BLOCK = 64
LANES = 128
PAIRS = BLOCK * BLOCK // LANES
GROUP = 16
HALF = PAIRS // 2
SIZE = PAIRS * GROUP
WIDTH = 1024
BOTH = ("row", "col")
NT = (((1,), (1,)), ((), ()))
NN = (((1,), (0,)), ((), ()))
F32 = jnp.float32
BF16 = jnp.bfloat16


def params(mib):
    return pltpu.CompilerParams(vmem_limit_bytes=mib << 20)


def dot(a, b, dims=NN):
    return lax.dot_general(a, b, dims, preferred_element_type=F32)


def as_ones(mask):
    return jnp.where(mask, 1.0, 0.0).astype(BF16)


def gathered(base_ref, index, piece_refs):
    shape = (piece_refs[0].shape[1], index.shape[1])
    place = index - lax.broadcasted_iota(jnp.int32, shape, 0)
    total = None
    for d, piece in enumerate(piece_refs):
        part = dot(piece[...], as_ones(place == base_ref[d]))
        total = part if total is None else total + part
    return total


def masked(index, count):
    return jnp.where(lax.broadcasted_iota(jnp.int32, index.shape, 1) < count, index, -1)


def early_kernel(base_ref, count_ref, far_ref, own_ref, *refs):
    pieces, (tile_ref, picked_ref, x_ref, far_order_ref, held_ref, sem) = refs[:-6], refs[-6:]
    copy = pltpu.make_async_copy(tile_ref, held_ref, sem)
    copy.start()
    far_order_ref[...] = turned_slots(far_ref[...])
    picked_ref[...] = gathered(base_ref, far_ref[...], pieces).astype(BF16)
    own_order = turned_slots(masked(own_ref[...], count_ref[0]))
    x_ref[...] = gathered(base_ref, own_order, pieces).astype(BF16)
    copy.wait()


def early_pick(bases, used, far_index, own_index, pieces, tile):
    whole = pl.BlockSpec(memory_space=pltpu.VMEM)
    shape = jax.ShapeDtypeStruct((pieces[0].shape[0], far_index.shape[1]), BF16)
    return pl.pallas_call(
        early_kernel,
        out_shape=(
            shape,
            shape,
            jax.ShapeDtypeStruct(far_index.shape, far_index.dtype),
            jax.ShapeDtypeStruct(tile.shape, tile.dtype),
        ),
        in_specs=[pl.BlockSpec(memory_space=pltpu.SMEM)] * 2
        + [whole] * (2 + len(pieces))
        + [pl.BlockSpec(memory_space=pl.ANY)],
        out_specs=(whole,) * 4,
        scratch_shapes=[pltpu.SemaphoreType.DMA],
        compiler_params=params(42),
        name="early_pick",
    )(bases, used, far_index, own_index, *pieces, tile)


def pick_kernel(base_ref, index_ref, before_ref, *refs):
    total = gathered(base_ref, index_ref[...], refs[:-1])
    refs[-1][...] = (before_ref[...].astype(F32) + total).astype(BF16)


def pick(bases, index, before, pieces):
    whole = pl.BlockSpec(memory_space=pltpu.VMEM)
    return pl.pallas_call(
        pick_kernel,
        out_shape=jax.ShapeDtypeStruct(before.shape, BF16),
        in_specs=[pl.BlockSpec(memory_space=pltpu.SMEM)] + [whole] * (2 + len(pieces)),
        out_specs=whole,
        compiler_params=params(16),
        name="pick",
    )(bases, index, before, *pieces)


def order_matrix(vecs):
    place = np.arange(vecs * BLOCK)
    pair, kind = place // GROUP, place % GROUP
    half, k, parity = kind // (2 * vecs), kind % (2 * vecs) // 2, kind % 2
    entry = k * BLOCK + 2 * (half * HALF + pair) + parity
    return jnp.asarray(np.arange(vecs * BLOCK)[:, None] == entry, BF16)


def route_matrix(vecs):
    row = np.arange(2 * vecs * SIZE)[:, None]
    kind, pair = row // SIZE, row % SIZE // GROUP
    return jnp.asarray(np.arange(vecs * BLOCK) == kind // 2 * BLOCK + 2 * pair + kind % 2, BF16)


def turned_slots(index):
    lane = lax.broadcasted_iota(jnp.int32, (1, LANES), 1)
    parts = []
    for n in range(index.shape[1] // LANES):
        part = index[:, n * LANES : (n + 1) * LANES]
        for bit in (1, 2, 4, 8):
            part = jnp.where(lane & bit != 0, pltpu.roll(part, bit, 1), pltpu.roll(part, LANES - bit, 1))
        parts.append(part)
    return jnp.concatenate(parts, 1)


def stacked(tile_ref, at, half):
    parts = [tile_ref[at, c * LANES : (c + 1) * LANES] for c in range(half * HALF, (half + 1) * HALF)]
    return jnp.concatenate(parts, 0)


def forward_kernel(vecs, base_ref, count_ref, index_ref, before_ref, *refs):
    pieces, (order_ref, tile_ref, out_ref, x_ref, packed_ref) = refs[:-5], refs[-5:]
    own_order = turned_slots(masked(index_ref[...], count_ref[0]))
    x_ref[...] = (before_ref[...].astype(F32) + gathered(base_ref, own_order, pieces)).T
    lane = lax.broadcasted_iota(jnp.int32, (GROUP, LANES), 1)
    row = lax.broadcasted_iota(jnp.int32, (GROUP, LANES), 0)
    first = lane < BLOCK
    masks = [as_ones((lane + row + 1) % GROUP == n) for n in range(GROUP)]

    def step(g, _):
        at = pl.ds(pl.multiple_of(g * GROUP, GROUP), GROUP)
        rows = []
        for p in range(vecs // 2):
            both = x_ref[at, p * LANES : (p + 1) * LANES]
            swapped = pltpu.roll(both, BLOCK, 1)
            rows += [
                jnp.where(first, both, 0.0),
                jnp.where(first, 0.0, swapped),
                jnp.where(first, swapped, 0.0),
                jnp.where(first, 0.0, both),
            ]
        left = jnp.concatenate(rows, 0).astype(BF16)
        packed = [[], []]
        for half in range(2):
            out = dot(left, stacked(tile_ref, at, half), NT).astype(BF16)
            for s in range(2 * vecs):
                shift = half * 2 * vecs + s
                for v in range(2):
                    part = out[s * GROUP : (s + 1) * GROUP, v * LANES : (v + 1) * LANES]
                    packed[v].append((pltpu.roll(part, shift, 1) if shift else part) * masks[shift])
        for v in range(2):
            part = sum(packed[v][1:], packed[v][0]).astype(F32)
            part = pltpu.roll(part, LANES + 1 - GROUP, 1, stride=1, stride_axis=0)
            packed_ref[at, v * LANES : (v + 1) * LANES] = part.astype(BF16)
        return 0

    lax.fori_loop(0, x_ref.shape[0] // GROUP, step, 0, unroll=32)
    out_ref[...] = dot(packed_ref[...], order_ref[...], NT).astype(BF16)


def forward(vecs, bases, used, index, before, pieces, order, tile):
    slots, wide = tile.shape[0], vecs * BLOCK
    whole = pl.BlockSpec(memory_space=pltpu.VMEM)
    return pl.pallas_call(
        functools.partial(forward_kernel, vecs),
        out_shape=jax.ShapeDtypeStruct((slots, wide), BF16),
        in_specs=[pl.BlockSpec(memory_space=pltpu.SMEM)] * 2 + [whole] * (len(pieces) + 4),
        out_specs=whole,
        scratch_shapes=[
            pltpu.VMEM((slots, wide), F32),
            pltpu.VMEM((slots, wide), BF16),
        ],
        compiler_params=params(20),
        name="forward",
    )(bases, used, index, before, *pieces, order, tile)


def backward_kernel(vecs, y_ref, route_ref, tile_ref, out_ref, wide_ref):
    shape = (out_ref.shape[0], SIZE)
    own = (
        lax.broadcasted_iota(jnp.int32, shape, 1) % GROUP == lax.broadcasted_iota(jnp.int32, shape, 0) % GROUP
    )
    far = y_ref[...].astype(F32).T.astype(BF16)
    for s in range(2 * vecs):
        part = dot(far, route_ref[s * SIZE : (s + 1) * SIZE, :], NT)
        wide_ref[:, s * SIZE : (s + 1) * SIZE] = jnp.where(own, part, 0.0).astype(BF16)
    first = lax.broadcasted_iota(jnp.int32, (GROUP, LANES), 1) < BLOCK
    span = HALF * GROUP

    def step(g, _):
        at = pl.ds(pl.multiple_of(g * GROUP, GROUP), GROUP)
        out = None
        for half in range(2):
            left = [
                wide_ref[at, s * SIZE + half * span : s * SIZE + (half + 1) * span] for s in range(2 * vecs)
            ]
            part = dot(jnp.concatenate(left, 0), stacked(tile_ref, at, half))
            out = part if out is None else out + part
        sums = []
        for k in range(vecs):
            even, odd = out[2 * k * GROUP : (2 * k + 1) * GROUP], out[(2 * k + 1) * GROUP : (2 * k + 2) * GROUP]
            part = jnp.where(first, even, odd)
            sums.append(part + pltpu.roll(part, BLOCK, 1))
        for p in range(vecs // 2):
            out_ref[at, p * LANES : (p + 1) * LANES] = jnp.where(first, sums[2 * p], sums[2 * p + 1]).astype(BF16)
        return 0

    lax.fori_loop(0, out_ref.shape[0] // GROUP, step, 0, unroll=32)


def backward(vecs, far, route, tile):
    wide, slots = far.shape
    whole = pl.BlockSpec(memory_space=pltpu.VMEM)
    return pl.pallas_call(
        functools.partial(backward_kernel, vecs),
        out_shape=jax.ShapeDtypeStruct((slots, wide), BF16),
        in_specs=[whole] * 3,
        out_specs=whole,
        scratch_shapes=[
            pltpu.VMEM((slots, 2 * vecs * SIZE), BF16),
        ],
        compiler_params=params(20),
        name="backward",
    )(far, route, tile)


def spread_kernel(count_ref, index_ref, part_ref, *refs):
    before, out_ref = refs[:-1], refs[-1]
    count = out_ref.shape[0]
    base = pl.program_id(0) * count
    place = lax.broadcasted_iota(jnp.int32, (count, index_ref.shape[1]), 0) + base
    total = dot(as_ones(place == masked(index_ref[...], count_ref[0])), part_ref[...])
    for more in before:
        total += more[pl.ds(pl.multiple_of(base, count), count), :]
    out_ref[...] = total.astype(out_ref.dtype)


def spread(used, index, part, blocks, dtype, *before):
    whole = pl.BlockSpec(memory_space=pltpu.VMEM)
    return pl.pallas_call(
        spread_kernel,
        grid=(blocks // WIDTH,),
        out_shape=jax.ShapeDtypeStruct((blocks, part.shape[1]), dtype),
        in_specs=[pl.BlockSpec(memory_space=pltpu.SMEM)] + [whole] * (2 + len(before)),
        out_specs=pl.BlockSpec((WIDTH, part.shape[1]), lambda i: (i, 0)),
        compiler_params=params(20),
        name="spread",
    )(used, index, part, *before)


def total_kernel(vecs, part_ref, vector_ref, early_ref, sum_ref, gram_ref):
    total = part_ref[0].astype(F32)
    for n in range(1, part_ref.shape[0]):
        total += part_ref[n].astype(F32)
    sum_ref[...] = total
    lines = []
    for p in range(3 * vecs // 2):
        pair = vector_ref[:, p * LANES : (p + 1) * LANES]
        swapped = pltpu.roll(pair, BLOCK, 1)
        for q in range(vecs // 2):
            both = total[:, q * LANES : (q + 1) * LANES]
            lines += [(pair * both).sum(0, keepdims=True), (swapped * both).sum(0, keepdims=True)]
    lines = jnp.concatenate(lines, 0)
    shape = lines.shape
    row = lax.broadcasted_iota(jnp.int32, shape, 0)
    lane = lax.broadcasted_iota(jnp.int32, shape, 1)
    swap, q, p = row % 2, row // 2 % (vecs // 2), row // vecs
    even = (2 * p + swap) * vecs + 2 * q
    odd = (2 * p + 1 - swap) * vecs + 2 * q + 1
    late = jnp.where(lane == even, lines[:, :BLOCK].sum(1, keepdims=True), 0.0)
    late += jnp.where(lane == odd, lines[:, BLOCK:].sum(1, keepdims=True), 0.0)
    packed = jnp.concatenate([early_ref[...], late.sum(0, keepdims=True)], 0)
    gram_ref[...] = jnp.broadcast_to(packed[None], gram_ref.shape)


def totalled(vecs, parts, vectors, early, peers):
    whole = pl.BlockSpec(memory_space=pltpu.VMEM)
    return pl.pallas_call(
        functools.partial(total_kernel, vecs),
        out_shape=(
            jax.ShapeDtypeStruct(parts.shape[1:], F32),
            jax.ShapeDtypeStruct((peers, early.shape[0] + 1, LANES), F32),
        ),
        in_specs=[whole] * 3,
        out_specs=(whole, whole),
        compiler_params=params(12),
        name="totalled",
    )(parts, vectors, early)


def unpack_kernel(vecs, scale, gram_ref, a_ref, b_ref):
    packed = gram_ref[0]
    for n in range(1, gram_ref.shape[0]):
        packed += gram_ref[n]
    packed = packed * scale
    wide, half = 5 * vecs, 3 * vecs // 2
    lane = lax.broadcasted_iota(jnp.int32, (1, LANES), 1)

    def shifted(line, by):
        by = by % LANES
        return pltpu.roll(packed[line : line + 1], by, 1) if by else packed[line : line + 1]

    for m in range(3 * vecs):
        line, at = m // half, m % half * wide
        b_ref[m : m + 1, :] = shifted(line, -at)[:, : 3 * vecs]
        first, last = shifted(line, -at - 3 * vecs), shifted(line, -at - 2 * vecs)
        middle = shifted(2, vecs - m * vecs)
        mixed = jnp.where(lane < vecs, first, jnp.where(lane < 2 * vecs, middle, last))
        a_ref[m : m + 1, :] = mixed[:, : 3 * vecs]


def unpacked(vecs, gram, scale):
    whole = pl.BlockSpec(memory_space=pltpu.VMEM)
    shape = jax.ShapeDtypeStruct((3 * vecs, 3 * vecs), F32)
    return pl.pallas_call(
        functools.partial(unpack_kernel, vecs, scale),
        out_shape=(shape, shape),
        in_specs=[whole],
        out_specs=(whole, whole),
        compiler_params=params(12),
        name="unpacked",
    )(gram)


def body(x_vec, hx_vec, p_vec, hp_vec, theta, precond, tile_vals, tile_rows, tile_cols, tile_count):
    vecs, piece_len = x_vec.shape
    rows, cols = lax.axis_size("row"), lax.axis_size("col")
    ring = rows // 2
    ndim_total = piece_len * rows * cols
    row_pos = lax.axis_index("row")
    width = piece_len // BLOCK
    slots = tile_vals.shape[2]
    tile = tile_vals[0, 0]
    residue = (hx_vec - x_vec * theta[:, None]) / precond[None, :]
    live = jnp.arange(slots, dtype=jnp.int32) < tile_count[0, 0]
    row_index = jnp.where(live, tile_rows[0, 0], -1)[None]
    col_index = tile_cols[0, 0][None]
    used = tile_count.reshape(1)

    def along(block, sign):
        path = [(r * cols + c, r * cols + (c + sign * r) % cols) for r in range(rows) for c in range(cols)]
        return lax.ppermute(block, BOTH, path)

    def within(block, flip, turn):
        return lax.ppermute(
            block, "row", [(i, (i // ring ^ flip) * ring + (i % ring + turn) % ring) for i in range(rows)]
        )

    own = residue.astype(BF16).reshape(vecs, width, BLOCK).transpose(0, 2, 1).reshape(vecs * BLOCK, width)
    across = within(own, 1, 0)
    pieces = [own, across] + [within(own, 0, n) for n in (1, 3, 2)]
    pieces += [within(across, 0, n) for n in (1, 3, 2)]
    flips = jnp.array([0, 1, 0, 0, 0, 1, 1, 1], jnp.int32)
    turns = jnp.array([0, 0, 1, 3, 2, 1, 3, 2], jnp.int32)
    bases = width * ((row_pos // ring ^ flips) * ring + (row_pos % ring - turns) % ring)
    far_index = along(lax.optimization_barrier((row_index, pieces[2]))[0], 1)
    near = 5
    picked, x_slots, far_order, held = early_pick(
        bases[:near], used, far_index, col_index, pieces[:near], tile
    )
    far = along(pick(bases[near:], far_index, picked, pieces[near:]), -1)
    forth = forward(vecs, bases[near:], used, col_index, x_slots, pieces[near:], order_matrix(vecs), held)
    forth = along(forth, 1)
    back = backward(vecs, far, route_matrix(vecs), held)
    back = spread(used, col_index, back, rows * width, F32)
    every = jnp.full((1,), slots, jnp.int32)
    parts = spread(every, far_order, forth, rows * width, BF16, back).reshape(rows, width, vecs * BLOCK)
    parts = lax.all_to_all(parts, "row", 0, 0, tiled=True)
    vectors = jnp.concatenate([x_vec, residue, p_vec], 0)
    known = jnp.concatenate([vectors, hx_vec, hp_vec], 0)
    early = jnp.dot(vectors, known.T, precision=lax.Precision.HIGHEST, preferred_element_type=F32)
    early = early.reshape(2, -1)
    early = jnp.pad(early, ((0, 0), (0, LANES - early.shape[1])))
    blocked = vectors.reshape(-1, width, BLOCK).transpose(1, 0, 2).reshape(width, -1)
    total, gram = totalled(vecs, parts, blocked, early, rows * cols)
    hw_vec = total.reshape(width, vecs, BLOCK).transpose(1, 0, 2).reshape(vecs, piece_len)
    gram = lax.all_to_all(gram, BOTH, 0, 0, tiled=True)
    gram_a, gram_b = unpacked(vecs, gram, 1.0 / ndim_total)
    return hw_vec, gram_a, gram_b


def solution(mesh):
    vector = P(None, ("col", "row"))
    placed = (
        vector,
        vector,
        vector,
        vector,
        P(),
        P(("col", "row")),
        P("row", "col", None, None),
        P("row", "col", None),
        P("row", "col", None),
        P("row", "col"),
    )
    return jax.shard_map(body, mesh=mesh, in_specs=placed, out_specs=(vector, P(), P()), check_vma=False)
```

```python
import functools

import jax
import jax.numpy as jnp
import numpy as np
from jax import lax
from jax.experimental import pallas as pl
from jax.experimental.pallas import tpu as pltpu
from jax.sharding import PartitionSpec as P

BLOCK = 64
LANES = 128
PAIRS = BLOCK * BLOCK // LANES
GROUP = 16
HALF = PAIRS // 2
SIZE = PAIRS * GROUP
WIDTH = 1024
COPIES = 8
BOTH = ("row", "col")
NT = (((1,), (1,)), ((), ()))
NN = (((1,), (0,)), ((), ()))
F32 = jnp.float32
BF16 = jnp.bfloat16


def params(mib):
    return pltpu.CompilerParams(vmem_limit_bytes=mib << 20)


def dot(a, b, dims=NN):
    return lax.dot_general(a, b, dims, preferred_element_type=F32)


def as_ones(mask):
    return jnp.where(mask, 1.0, 0.0).astype(BF16)


def gathered(base_ref, index, piece_refs):
    shape = (piece_refs[0].shape[1], index.shape[1])
    place = index - lax.broadcasted_iota(jnp.int32, shape, 0)
    total = None
    for d, piece in enumerate(piece_refs):
        part = dot(piece[...], as_ones(place == base_ref[d]))
        total = part if total is None else total + part
    return total


def masked(index, count):
    return jnp.where(lax.broadcasted_iota(jnp.int32, index.shape, 1) < count, index, -1)


def early_kernel(base_ref, count_ref, own_ref, *refs):
    pieces, (tile_ref, x_ref, held_ref, sems) = refs[:-4], refs[-4:]
    size = held_ref.shape[0] // COPIES
    copies = []
    for n in range(COPIES):
        at = pl.ds(n * size, size)
        copies.append(pltpu.make_async_copy(tile_ref.at[at], held_ref.at[at], sems.at[n]))
        copies[-1].start()
    own_order = turned_slots(masked(own_ref[...], count_ref[0]))
    x_ref[...] = gathered(base_ref, own_order, pieces).astype(BF16)
    for copy in copies:
        copy.wait()


def early_pick(bases, used, own_index, pieces, tile):
    whole = pl.BlockSpec(memory_space=pltpu.VMEM)
    return pl.pallas_call(
        early_kernel,
        out_shape=(
            jax.ShapeDtypeStruct((pieces[0].shape[0], own_index.shape[1]), BF16),
            jax.ShapeDtypeStruct((tile.shape[0] // 2, tile.shape[1]), tile.dtype),
        ),
        in_specs=[pl.BlockSpec(memory_space=pltpu.SMEM)] * 2
        + [whole] * (1 + len(pieces))
        + [pl.BlockSpec(memory_space=pl.ANY)],
        out_specs=(whole,) * 2,
        scratch_shapes=[pltpu.SemaphoreType.DMA((COPIES,))],
        compiler_params=params(42),
        name="early_pick",
    )(bases, used, own_index, *pieces, tile)


def pick_kernel(base_ref, index_ref, *refs):
    pieces, (out_ref, order_ref) = refs[:-2], refs[-2:]
    order_ref[...] = turned_slots(index_ref[...])
    out_ref[...] = gathered(base_ref, index_ref[...], pieces).astype(BF16)


def pick(bases, index, pieces):
    whole = pl.BlockSpec(memory_space=pltpu.VMEM)
    return pl.pallas_call(
        pick_kernel,
        out_shape=(
            jax.ShapeDtypeStruct((pieces[0].shape[0], index.shape[1]), BF16),
            jax.ShapeDtypeStruct(index.shape, index.dtype),
        ),
        in_specs=[pl.BlockSpec(memory_space=pltpu.SMEM)] + [whole] * (1 + len(pieces)),
        out_specs=(whole,) * 2,
        compiler_params=params(16),
        name="pick",
    )(bases, index, *pieces)


def order_matrix(vecs):
    place = np.arange(vecs * BLOCK)
    pair, kind = place // GROUP, place % GROUP
    half, k, parity = kind // (2 * vecs), kind % (2 * vecs) // 2, kind % 2
    entry = k * BLOCK + 2 * (half * HALF + pair) + parity
    return jnp.asarray(np.arange(vecs * BLOCK)[:, None] == entry, BF16)


def route_matrix(vecs):
    row = np.arange(2 * vecs * SIZE)[:, None]
    kind, pair = row // SIZE, row % SIZE // GROUP
    return jnp.asarray(np.arange(vecs * BLOCK) == kind // 2 * BLOCK + 2 * pair + kind % 2, BF16)


def turned_slots(index):
    lane = lax.broadcasted_iota(jnp.int32, (1, LANES), 1)
    parts = []
    for n in range(index.shape[1] // LANES):
        part = index[:, n * LANES : (n + 1) * LANES]
        for bit in (1, 2, 4, 8):
            part = jnp.where(lane & bit != 0, pltpu.roll(part, bit, 1), pltpu.roll(part, LANES - bit, 1))
        parts.append(part)
    return jnp.concatenate(parts, 1)


def stacked(tile_ref, at, half):
    parts = [tile_ref[at, c * LANES : (c + 1) * LANES] for c in range(half * HALF, (half + 1) * HALF)]
    return jnp.concatenate(parts, 0)


def forward_kernel(vecs, base_ref, count_ref, index_ref, before_ref, *refs):
    pieces, (order_ref, half_ref, tile_ref, out_ref, rest_ref, x_ref, packed_ref, sem) = refs[:-8], refs[-8:]
    size = rest_ref.shape[0]
    copy = pltpu.make_async_copy(tile_ref.at[pl.ds(size, size)], rest_ref, sem)
    copy.start()
    own_order = turned_slots(masked(index_ref[...], count_ref[0]))
    x_ref[...] = (before_ref[...].astype(F32) + gathered(base_ref, own_order, pieces)).T
    lane = lax.broadcasted_iota(jnp.int32, (GROUP, LANES), 1)
    row = lax.broadcasted_iota(jnp.int32, (GROUP, LANES), 0)
    first = lane < BLOCK
    masks = [as_ones((lane + row + 1) % GROUP == n) for n in range(GROUP)]

    def step(held_ref, base, g, _):
        at = pl.ds(pl.multiple_of(base + g * GROUP, GROUP), GROUP)
        here = pl.ds(pl.multiple_of(g * GROUP, GROUP), GROUP)
        rows = []
        for p in range(vecs // 2):
            both = x_ref[at, p * LANES : (p + 1) * LANES]
            swapped = pltpu.roll(both, BLOCK, 1)
            rows += [
                jnp.where(first, both, 0.0),
                jnp.where(first, 0.0, swapped),
                jnp.where(first, swapped, 0.0),
                jnp.where(first, 0.0, both),
            ]
        left = jnp.concatenate(rows, 0).astype(BF16)
        packed = [[], []]
        for half in range(2):
            out = dot(left, stacked(held_ref, here, half), NT).astype(BF16)
            for s in range(2 * vecs):
                shift = half * 2 * vecs + s
                for v in range(2):
                    part = out[s * GROUP : (s + 1) * GROUP, v * LANES : (v + 1) * LANES]
                    packed[v].append((pltpu.roll(part, shift, 1) if shift else part) * masks[shift])
        for v in range(2):
            part = sum(packed[v][1:], packed[v][0]).astype(F32)
            part = pltpu.roll(part, LANES + 1 - GROUP, 1, stride=1, stride_axis=0)
            packed_ref[at, v * LANES : (v + 1) * LANES] = part.astype(BF16)
        return 0

    lax.fori_loop(0, size // GROUP, functools.partial(step, half_ref, 0), 0, unroll=32)
    copy.wait()
    lax.fori_loop(0, size // GROUP, functools.partial(step, rest_ref, size), 0, unroll=32)
    out_ref[...] = dot(packed_ref[...], order_ref[...], NT).astype(BF16)


def forward(vecs, bases, used, index, before, pieces, order, half, tile):
    slots, wide = tile.shape[0], vecs * BLOCK
    whole = pl.BlockSpec(memory_space=pltpu.VMEM)
    return pl.pallas_call(
        functools.partial(forward_kernel, vecs),
        out_shape=(
            jax.ShapeDtypeStruct((slots, wide), BF16),
            jax.ShapeDtypeStruct((slots - half.shape[0], tile.shape[1]), tile.dtype),
        ),
        in_specs=[pl.BlockSpec(memory_space=pltpu.SMEM)] * 2
        + [whole] * (len(pieces) + 4)
        + [pl.BlockSpec(memory_space=pl.ANY)],
        out_specs=(whole,) * 2,
        scratch_shapes=[
            pltpu.VMEM((slots, wide), F32),
            pltpu.VMEM((slots, wide), BF16),
            pltpu.SemaphoreType.DMA,
        ],
        compiler_params=params(42),
        name="forward",
    )(bases, used, index, before, *pieces, order, half, tile)


def backward_kernel(vecs, y_ref, route_ref, half_ref, rest_ref, out_ref, wide_ref):
    shape = (out_ref.shape[0], SIZE)
    own = (
        lax.broadcasted_iota(jnp.int32, shape, 1) % GROUP == lax.broadcasted_iota(jnp.int32, shape, 0) % GROUP
    )
    far = y_ref[...].astype(F32).T.astype(BF16)
    for s in range(2 * vecs):
        part = dot(far, route_ref[s * SIZE : (s + 1) * SIZE, :], NT)
        wide_ref[:, s * SIZE : (s + 1) * SIZE] = jnp.where(own, part, 0.0).astype(BF16)
    first = lax.broadcasted_iota(jnp.int32, (GROUP, LANES), 1) < BLOCK
    span = HALF * GROUP

    def step(held_ref, base, g, _):
        at = pl.ds(pl.multiple_of(base + g * GROUP, GROUP), GROUP)
        here = pl.ds(pl.multiple_of(g * GROUP, GROUP), GROUP)
        out = None
        for half in range(2):
            left = [
                wide_ref[at, s * SIZE + half * span : s * SIZE + (half + 1) * span] for s in range(2 * vecs)
            ]
            part = dot(jnp.concatenate(left, 0), stacked(held_ref, here, half))
            out = part if out is None else out + part
        sums = []
        for k in range(vecs):
            even, odd = out[2 * k * GROUP : (2 * k + 1) * GROUP], out[(2 * k + 1) * GROUP : (2 * k + 2) * GROUP]
            part = jnp.where(first, even, odd)
            sums.append(part + pltpu.roll(part, BLOCK, 1))
        for p in range(vecs // 2):
            out_ref[at, p * LANES : (p + 1) * LANES] = jnp.where(first, sums[2 * p], sums[2 * p + 1]).astype(BF16)
        return 0

    size = half_ref.shape[0]
    for n, held_ref in enumerate((half_ref, rest_ref)):
        lax.fori_loop(0, size // GROUP, functools.partial(step, held_ref, n * size), 0, unroll=32)


def backward(vecs, far, route, half, rest):
    wide, slots = far.shape
    whole = pl.BlockSpec(memory_space=pltpu.VMEM)
    return pl.pallas_call(
        functools.partial(backward_kernel, vecs),
        out_shape=jax.ShapeDtypeStruct((slots, wide), BF16),
        in_specs=[whole] * 4,
        out_specs=whole,
        scratch_shapes=[
            pltpu.VMEM((slots, 2 * vecs * SIZE), BF16),
        ],
        compiler_params=params(20),
        name="backward",
    )(far, route, half, rest)


def spread_kernel(count_ref, index_ref, part_ref, *refs):
    before, out_ref = refs[:-1], refs[-1]
    count = out_ref.shape[0]
    base = pl.program_id(0) * count
    place = lax.broadcasted_iota(jnp.int32, (count, index_ref.shape[1]), 0) + base
    total = dot(as_ones(place == masked(index_ref[...], count_ref[0])), part_ref[...])
    for more in before:
        total += more[pl.ds(pl.multiple_of(base, count), count), :]
    out_ref[...] = total.astype(out_ref.dtype)


def spread(used, index, part, blocks, dtype, *before):
    whole = pl.BlockSpec(memory_space=pltpu.VMEM)
    return pl.pallas_call(
        spread_kernel,
        grid=(blocks // WIDTH,),
        out_shape=jax.ShapeDtypeStruct((blocks, part.shape[1]), dtype),
        in_specs=[pl.BlockSpec(memory_space=pltpu.SMEM)] + [whole] * (2 + len(before)),
        out_specs=pl.BlockSpec((WIDTH, part.shape[1]), lambda i: (i, 0)),
        compiler_params=params(20),
        name="spread",
    )(used, index, part, *before)


def early_kernel_gram(vecs, *refs):
    vectors, (out_ref, held_ref) = refs[:-2], refs[-2:]
    for n, vector in enumerate(vectors):
        held_ref[n * vecs : (n + 1) * vecs, :] = vector[...]
    left, right = held_ref[: 3 * vecs, :], held_ref[...]
    gram = lax.dot_general(left, right, NT, precision=lax.Precision.HIGHEST, preferred_element_type=F32)
    rows = [gram[m : m + 1, m // vecs * vecs :] for m in range(3 * vecs)]
    for line, some in enumerate((rows[:vecs], rows[vecs:])):
        blank = jnp.zeros((1, LANES - sum(row.shape[1] for row in some)), F32)
        out_ref[line : line + 1, :] = jnp.concatenate(some + [blank], 1)


def early_gram(vecs, *vectors):
    whole = pl.BlockSpec(memory_space=pltpu.VMEM)
    return pl.pallas_call(
        functools.partial(early_kernel_gram, vecs),
        out_shape=jax.ShapeDtypeStruct((2, LANES), F32),
        in_specs=[whole] * len(vectors),
        out_specs=whole,
        scratch_shapes=[pltpu.VMEM((vecs * len(vectors), vectors[0].shape[1]), F32)],
        compiler_params=params(16),
        name="early_gram",
    )(*vectors)


def total_kernel(vecs, part_ref, vector_ref, early_ref, sum_ref, gram_ref):
    total = part_ref[0].astype(F32)
    for n in range(1, part_ref.shape[0]):
        total += part_ref[n].astype(F32)
    sum_ref[...] = total
    lines = []
    for p in range(3 * vecs // 2):
        pair = vector_ref[:, p * LANES : (p + 1) * LANES]
        swapped = pltpu.roll(pair, BLOCK, 1)
        for q in range(vecs // 2):
            both = total[:, q * LANES : (q + 1) * LANES]
            lines += [(pair * both).sum(0, keepdims=True), (swapped * both).sum(0, keepdims=True)]
    lines = jnp.concatenate(lines, 0)
    shape = lines.shape
    row = lax.broadcasted_iota(jnp.int32, shape, 0)
    lane = lax.broadcasted_iota(jnp.int32, shape, 1)
    swap, q, p = row % 2, row // 2 % (vecs // 2), row // vecs
    first = 5 * vecs * vecs
    even = first + (2 * p + swap) * vecs + 2 * q
    odd = first + (2 * p + 1 - swap) * vecs + 2 * q + 1
    late = jnp.where(lane == even, lines[:, :BLOCK].sum(1, keepdims=True), 0.0)
    late += jnp.where(lane == odd, lines[:, BLOCK:].sum(1, keepdims=True), 0.0)
    late = late.sum(0, keepdims=True)
    packed = early_ref[...] + jnp.concatenate([late, jnp.zeros_like(late)], 0)
    gram_ref[...] = jnp.broadcast_to(packed[None], gram_ref.shape)


def totalled(vecs, parts, vectors, early, peers):
    whole = pl.BlockSpec(memory_space=pltpu.VMEM)
    return pl.pallas_call(
        functools.partial(total_kernel, vecs),
        out_shape=(
            jax.ShapeDtypeStruct(parts.shape[1:], F32),
            jax.ShapeDtypeStruct((peers, *early.shape), F32),
        ),
        in_specs=[whole] * 3,
        out_specs=(whole, whole),
        compiler_params=params(12),
        name="totalled",
    )(parts, vectors, early)


def unpack_kernel(vecs, scale, gram_ref, a_ref, b_ref):
    packed = gram_ref[0]
    for n in range(1, gram_ref.shape[0]):
        packed += gram_ref[n]
    packed = packed * scale
    lane = lax.broadcasted_iota(jnp.int32, (1, LANES), 1)
    late = 5 * vecs * vecs

    def assembled(runs):
        out = jnp.zeros((1, LANES), F32)
        for line, source, to, count in runs:
            by = (to - source) % LANES
            moved = packed[line : line + 1]
            moved = pltpu.roll(moved, by, 1) if by else moved
            out = jnp.where((lane >= to) & (lane < to + count), moved, out)
        return out[:, : 3 * vecs]

    def place(block, i, column):
        if block == 0:
            return 0, (5 * i + column) * vecs
        if block == 1:
            return 1, (4 * i + column - 1) * vecs
        return 1, (4 * vecs + 3 * i + column - 2) * vecs

    for m in range(3 * vecs):
        block, i = m // vecs, m % vecs
        runs = [(*place(block, i, column), column * vecs, vecs) for column in range(block, 3)]
        for column in range(block):
            for j in range(vecs):
                line, at = place(column, j, block)
                runs.append((line, at + i, column * vecs + j, 1))
        b_ref[m : m + 1, :] = assembled(runs)
        images = [(*place(block, i, 3), 0, vecs), (0, late + m * vecs, vecs, vecs)]
        a_ref[m : m + 1, :] = assembled(images + [(*place(block, i, 4), 2 * vecs, vecs)])


def unpacked(vecs, gram, scale):
    whole = pl.BlockSpec(memory_space=pltpu.VMEM)
    shape = jax.ShapeDtypeStruct((3 * vecs, 3 * vecs), F32)
    return pl.pallas_call(
        functools.partial(unpack_kernel, vecs, scale),
        out_shape=(shape, shape),
        in_specs=[whole],
        out_specs=(whole, whole),
        compiler_params=params(12),
        name="unpacked",
    )(gram)


def body(x_vec, hx_vec, p_vec, hp_vec, theta, precond, tile_vals, tile_rows, tile_cols, tile_count):
    vecs, piece_len = x_vec.shape
    rows, cols = lax.axis_size("row"), lax.axis_size("col")
    ring = rows // 2
    ndim_total = piece_len * rows * cols
    row_pos = lax.axis_index("row")
    width = piece_len // BLOCK
    slots = tile_vals.shape[2]
    tile = tile_vals[0, 0]
    residue = (hx_vec - x_vec * theta[:, None]) / precond[None, :]
    live = jnp.arange(slots, dtype=jnp.int32) < tile_count[0, 0]
    row_index = jnp.where(live, tile_rows[0, 0], -1)[None]
    col_index = tile_cols[0, 0][None]
    used = tile_count.reshape(1)

    def along(block, sign):
        path = [(r * cols + c, r * cols + (c + sign * r) % cols) for r in range(rows) for c in range(cols)]
        return lax.ppermute(block, BOTH, path)

    def within(block, flip, turn):
        return lax.ppermute(
            block, "row", [(i, (i // ring ^ flip) * ring + (i % ring + turn) % ring) for i in range(rows)]
        )

    own = residue.astype(BF16).reshape(vecs, width, BLOCK).transpose(0, 2, 1).reshape(vecs * BLOCK, width)
    across = within(own, 1, 0)
    pieces = [own, across] + [within(own, 0, n) for n in (1, 3, 2)]
    pieces += [within(across, 0, n) for n in (1, 3, 2)]
    order = jnp.arange(rows, dtype=jnp.int32)
    flips = sum(1 << n for n in (1, 5, 6, 7)) >> order & 1
    turns = sum(turn << 2 * n for n, turn in enumerate((0, 0, 1, 3, 2, 1, 3, 2))) >> 2 * order & 3
    bases = width * ((row_pos // ring ^ flips) * ring + (row_pos % ring + ring - turns) % ring)
    far_index = along(lax.optimization_barrier((row_index, pieces[2]))[0], 1)
    near = 5
    x_slots, held = early_pick(bases[:near], used, col_index, pieces[:near], tile)
    picked, far_order = pick(bases, far_index, pieces)
    far = along(picked, -1)
    forth, rest = forward(vecs, bases[near:], used, col_index, x_slots, pieces[near:], order_matrix(vecs), held, tile)
    forth = along(forth, 1)
    back = backward(vecs, far, route_matrix(vecs), held, rest)
    back = spread(used, col_index, back, rows * width, F32)
    every = jnp.full((1,), slots, jnp.int32)
    parts = spread(every, far_order, forth, rows * width, BF16, back).reshape(rows, width, vecs * BLOCK)
    vectors = jnp.concatenate([x_vec, residue, p_vec], 0)
    tied = lax.optimization_barrier((x_vec, residue, p_vec, hx_vec, hp_vec, parts))
    early = early_gram(vecs, *tied[:5])
    blocked = vectors.reshape(-1, width, BLOCK).transpose(1, 0, 2).reshape(width, -1)
    parts = lax.all_to_all(tied[5], "row", 0, 0, tiled=True)
    total, gram = totalled(vecs, parts, blocked, early, rows * cols)
    hw_vec = total.reshape(width, vecs, BLOCK).transpose(1, 0, 2).reshape(vecs, piece_len)
    gram = lax.all_to_all(gram, BOTH, 0, 0, tiled=True)
    gram_a, gram_b = unpacked(vecs, gram, 1.0 / ndim_total)
    return hw_vec, gram_a, gram_b


def solution(mesh):
    vector = P(None, ("col", "row"))
    placed = (
        vector,
        vector,
        vector,
        vector,
        P(),
        P(("col", "row")),
        P("row", "col", None, None),
        P("row", "col", None),
        P("row", "col", None),
        P("row", "col"),
    )
    return jax.shard_map(body, mesh=mesh, in_specs=placed, out_specs=(vector, P(), P()), check_vma=False)
```

```python
import functools

import jax
import jax.numpy as jnp
import numpy as np
from jax import lax
from jax.experimental import pallas as pl
from jax.experimental.pallas import tpu as pltpu
from jax.sharding import PartitionSpec as P

BLOCK = 64
LANES = 128
PAIRS = BLOCK * BLOCK // LANES
GROUP = 16
HALF = PAIRS // 2
SIZE = PAIRS * GROUP
WIDTH = 1024
COPIES = 8
BOTH = ("row", "col")
NT = (((1,), (1,)), ((), ()))
NN = (((1,), (0,)), ((), ()))
F32 = jnp.float32
BF16 = jnp.bfloat16


def params(mib):
    return pltpu.CompilerParams(vmem_limit_bytes=mib << 20)


def dot(a, b, dims=NN):
    return lax.dot_general(a, b, dims, preferred_element_type=F32)


def as_ones(mask):
    return jnp.where(mask, 1.0, 0.0).astype(BF16)


def gathered(base_ref, index, piece_refs):
    shape = (piece_refs[0].shape[1], index.shape[1])
    place = index - lax.broadcasted_iota(jnp.int32, shape, 0)
    total = None
    for d, piece in enumerate(piece_refs):
        part = dot(piece[...], as_ones(place == base_ref[d]))
        total = part if total is None else total + part
    return total


def masked(index, count):
    return jnp.where(lax.broadcasted_iota(jnp.int32, index.shape, 1) < count, index, -1)


def early_kernel(base_ref, count_ref, own_ref, *refs):
    pieces, (tile_ref, x_ref, held_ref, sems) = refs[:-4], refs[-4:]
    size = held_ref.shape[0] // COPIES
    copies = []
    for n in range(COPIES):
        at = pl.ds(n * size, size)
        copies.append(pltpu.make_async_copy(tile_ref.at[at], held_ref.at[at], sems.at[n]))
        copies[-1].start()
    own_order = turned_slots(masked(own_ref[...], count_ref[0]))
    x_ref[...] = gathered(base_ref, own_order, pieces).astype(BF16)
    for copy in copies:
        copy.wait()


def early_pick(bases, used, own_index, pieces, tile):
    whole = pl.BlockSpec(memory_space=pltpu.VMEM)
    return pl.pallas_call(
        early_kernel,
        out_shape=(
            jax.ShapeDtypeStruct((pieces[0].shape[0], own_index.shape[1]), BF16),
            jax.ShapeDtypeStruct((tile.shape[0] // 2, tile.shape[1]), tile.dtype),
        ),
        in_specs=[pl.BlockSpec(memory_space=pltpu.SMEM)] * 2
        + [whole] * (1 + len(pieces))
        + [pl.BlockSpec(memory_space=pl.ANY)],
        out_specs=(whole,) * 2,
        scratch_shapes=[pltpu.SemaphoreType.DMA((COPIES,))],
        compiler_params=params(42),
        name="early_pick",
    )(bases, used, own_index, *pieces, tile)


def pick_kernel(base_ref, index_ref, *refs):
    pieces, (out_ref, order_ref) = refs[:-2], refs[-2:]
    order_ref[...] = turned_slots(index_ref[...])
    out_ref[...] = gathered(base_ref, index_ref[...], pieces).astype(BF16)


def pick(bases, index, pieces):
    whole = pl.BlockSpec(memory_space=pltpu.VMEM)
    return pl.pallas_call(
        pick_kernel,
        out_shape=(
            jax.ShapeDtypeStruct((pieces[0].shape[0], index.shape[1]), BF16),
            jax.ShapeDtypeStruct(index.shape, index.dtype),
        ),
        in_specs=[pl.BlockSpec(memory_space=pltpu.SMEM)] + [whole] * (1 + len(pieces)),
        out_specs=(whole,) * 2,
        compiler_params=params(16),
        name="pick",
    )(bases, index, *pieces)


def order_matrix(vecs):
    place = np.arange(vecs * BLOCK)
    pair, kind = place // GROUP, place % GROUP
    half, k, parity = kind // (2 * vecs), kind % (2 * vecs) // 2, kind % 2
    entry = k * BLOCK + 2 * (half * HALF + pair) + parity
    return jnp.asarray(np.arange(vecs * BLOCK)[:, None] == entry, BF16)


def route_matrix(vecs):
    row = np.arange(2 * vecs * SIZE)[:, None]
    kind, pair = row // SIZE, row % SIZE // GROUP
    return jnp.asarray(np.arange(vecs * BLOCK) == kind // 2 * BLOCK + 2 * pair + kind % 2, BF16)


def turned_slots(index):
    lane = lax.broadcasted_iota(jnp.int32, (1, LANES), 1)
    parts = []
    for n in range(index.shape[1] // LANES):
        part = index[:, n * LANES : (n + 1) * LANES]
        for bit in (1, 2, 4, 8):
            part = jnp.where(lane & bit != 0, pltpu.roll(part, bit, 1), pltpu.roll(part, LANES - bit, 1))
        parts.append(part)
    return jnp.concatenate(parts, 1)


def stacked(tile_ref, at, half):
    parts = [tile_ref[at, c * LANES : (c + 1) * LANES] for c in range(half * HALF, (half + 1) * HALF)]
    return jnp.concatenate(parts, 0)


def forward_kernel(vecs, base_ref, count_ref, index_ref, before_ref, *refs):
    pieces, (order_ref, half_ref, tile_ref, out_ref, rest_ref, x_ref, packed_ref, sem) = refs[:-8], refs[-8:]
    size = rest_ref.shape[0]
    copy = pltpu.make_async_copy(tile_ref.at[pl.ds(size, size)], rest_ref, sem)
    copy.start()
    own_order = turned_slots(masked(index_ref[...], count_ref[0]))
    x_ref[...] = (before_ref[...].astype(F32) + gathered(base_ref, own_order, pieces)).T
    lane = lax.broadcasted_iota(jnp.int32, (GROUP, LANES), 1)
    row = lax.broadcasted_iota(jnp.int32, (GROUP, LANES), 0)
    first = lane < BLOCK
    masks = [as_ones((lane + row + 1) % GROUP == n) for n in range(GROUP)]

    def step(held_ref, base, g, _):
        at = pl.ds(pl.multiple_of(base + g * GROUP, GROUP), GROUP)
        here = pl.ds(pl.multiple_of(g * GROUP, GROUP), GROUP)
        rows = []
        for p in range(vecs // 2):
            both = x_ref[at, p * LANES : (p + 1) * LANES]
            swapped = pltpu.roll(both, BLOCK, 1)
            rows += [
                jnp.where(first, both, 0.0),
                jnp.where(first, 0.0, swapped),
                jnp.where(first, swapped, 0.0),
                jnp.where(first, 0.0, both),
            ]
        left = jnp.concatenate(rows, 0).astype(BF16)
        packed = [[], []]
        for half in range(2):
            out = dot(left, stacked(held_ref, here, half), NT).astype(BF16)
            for s in range(2 * vecs):
                shift = half * 2 * vecs + s
                for v in range(2):
                    part = out[s * GROUP : (s + 1) * GROUP, v * LANES : (v + 1) * LANES]
                    packed[v].append((pltpu.roll(part, shift, 1) if shift else part) * masks[shift])
        for v in range(2):
            part = sum(packed[v][1:], packed[v][0]).astype(F32)
            part = pltpu.roll(part, LANES + 1 - GROUP, 1, stride=1, stride_axis=0)
            packed_ref[at, v * LANES : (v + 1) * LANES] = part.astype(BF16)
        return 0

    lax.fori_loop(0, size // GROUP, functools.partial(step, half_ref, 0), 0, unroll=32)
    copy.wait()
    lax.fori_loop(0, size // GROUP, functools.partial(step, rest_ref, size), 0, unroll=32)
    out_ref[...] = dot(packed_ref[...], order_ref[...], NT).astype(BF16)


def forward(vecs, bases, used, index, before, pieces, order, half, tile):
    slots, wide = tile.shape[0], vecs * BLOCK
    whole = pl.BlockSpec(memory_space=pltpu.VMEM)
    return pl.pallas_call(
        functools.partial(forward_kernel, vecs),
        out_shape=(
            jax.ShapeDtypeStruct((slots, wide), BF16),
            jax.ShapeDtypeStruct((slots - half.shape[0], tile.shape[1]), tile.dtype),
        ),
        in_specs=[pl.BlockSpec(memory_space=pltpu.SMEM)] * 2
        + [whole] * (len(pieces) + 4)
        + [pl.BlockSpec(memory_space=pl.ANY)],
        out_specs=(whole,) * 2,
        scratch_shapes=[
            pltpu.VMEM((slots, wide), F32),
            pltpu.VMEM((slots, wide), BF16),
            pltpu.SemaphoreType.DMA,
        ],
        compiler_params=params(42),
        name="forward",
    )(bases, used, index, before, *pieces, order, half, tile)


def backward_kernel(vecs, y_ref, route_ref, half_ref, rest_ref, out_ref, wide_ref):
    shape = (out_ref.shape[0], SIZE)
    own = (
        lax.broadcasted_iota(jnp.int32, shape, 1) % GROUP == lax.broadcasted_iota(jnp.int32, shape, 0) % GROUP
    )
    far = y_ref[...].astype(F32).T.astype(BF16)
    for s in range(2 * vecs):
        part = dot(far, route_ref[s * SIZE : (s + 1) * SIZE, :], NT)
        wide_ref[:, s * SIZE : (s + 1) * SIZE] = jnp.where(own, part, 0.0).astype(BF16)
    first = lax.broadcasted_iota(jnp.int32, (GROUP, LANES), 1) < BLOCK
    span = HALF * GROUP

    def step(held_ref, base, g, _):
        at = pl.ds(pl.multiple_of(base + g * GROUP, GROUP), GROUP)
        here = pl.ds(pl.multiple_of(g * GROUP, GROUP), GROUP)
        out = None
        for half in range(2):
            left = [
                wide_ref[at, s * SIZE + half * span : s * SIZE + (half + 1) * span] for s in range(2 * vecs)
            ]
            part = dot(jnp.concatenate(left, 0), stacked(held_ref, here, half))
            out = part if out is None else out + part
        sums = []
        for k in range(vecs):
            even, odd = out[2 * k * GROUP : (2 * k + 1) * GROUP], out[(2 * k + 1) * GROUP : (2 * k + 2) * GROUP]
            part = jnp.where(first, even, odd)
            sums.append(part + pltpu.roll(part, BLOCK, 1))
        for p in range(vecs // 2):
            out_ref[at, p * LANES : (p + 1) * LANES] = jnp.where(first, sums[2 * p], sums[2 * p + 1]).astype(BF16)
        return 0

    size = half_ref.shape[0]
    for n, held_ref in enumerate((half_ref, rest_ref)):
        lax.fori_loop(0, size // GROUP, functools.partial(step, held_ref, n * size), 0, unroll=32)


def backward(vecs, far, route, half, rest):
    wide, slots = far.shape
    whole = pl.BlockSpec(memory_space=pltpu.VMEM)
    return pl.pallas_call(
        functools.partial(backward_kernel, vecs),
        out_shape=jax.ShapeDtypeStruct((slots, wide), BF16),
        in_specs=[whole] * 4,
        out_specs=whole,
        scratch_shapes=[
            pltpu.VMEM((slots, 2 * vecs * SIZE), BF16),
        ],
        compiler_params=params(20),
        name="backward",
    )(far, route, half, rest)


def spread_kernel(count_ref, index_ref, part_ref, *refs):
    before, out_ref = refs[:-1], refs[-1]
    count = out_ref.shape[0]
    base = pl.program_id(0) * count
    place = lax.broadcasted_iota(jnp.int32, (count, index_ref.shape[1]), 0) + base
    total = dot(as_ones(place == masked(index_ref[...], count_ref[0])), part_ref[...])
    for more in before:
        total += more[pl.ds(pl.multiple_of(base, count), count), :]
    out_ref[...] = total.astype(out_ref.dtype)


def spread(used, index, part, blocks, dtype, *before):
    whole = pl.BlockSpec(memory_space=pltpu.VMEM)
    return pl.pallas_call(
        spread_kernel,
        grid=(blocks // WIDTH,),
        out_shape=jax.ShapeDtypeStruct((blocks, part.shape[1]), dtype),
        in_specs=[pl.BlockSpec(memory_space=pltpu.SMEM)] + [whole] * (2 + len(before)),
        out_specs=pl.BlockSpec((WIDTH, part.shape[1]), lambda i: (i, 0)),
        compiler_params=params(20),
        name="spread",
    )(used, index, part, *before)


def early_kernel_gram(vecs, *refs):
    vectors, (out_ref, held_ref) = refs[:-2], refs[-2:]
    for n, vector in enumerate(vectors):
        held_ref[n * vecs : (n + 1) * vecs, :] = vector[...]
    left, right = held_ref[: 3 * vecs, :], held_ref[...]
    gram = lax.dot_general(left, right, NT, precision=lax.Precision.HIGHEST, preferred_element_type=F32)
    rows = [gram[m : m + 1, m // vecs * vecs :] for m in range(3 * vecs)]
    for line, some in enumerate((rows[:vecs], rows[vecs:])):
        blank = jnp.zeros((1, LANES - sum(row.shape[1] for row in some)), F32)
        out_ref[line : line + 1, :] = jnp.concatenate(some + [blank], 1)


def early_gram(vecs, *vectors):
    whole = pl.BlockSpec(memory_space=pltpu.VMEM)
    return pl.pallas_call(
        functools.partial(early_kernel_gram, vecs),
        out_shape=jax.ShapeDtypeStruct((2, LANES), F32),
        in_specs=[whole] * len(vectors),
        out_specs=whole,
        scratch_shapes=[pltpu.VMEM((vecs * len(vectors), vectors[0].shape[1]), F32)],
        compiler_params=params(16),
        name="early_gram",
    )(*vectors)


def total_kernel(vecs, part_ref, vector_ref, early_ref, sum_ref, gram_ref):
    total = part_ref[0].astype(F32)
    for n in range(1, part_ref.shape[0]):
        total += part_ref[n].astype(F32)
    sum_ref[...] = total
    lines = []
    for p in range(3 * vecs // 2):
        pair = vector_ref[:, p * LANES : (p + 1) * LANES]
        swapped = pltpu.roll(pair, BLOCK, 1)
        for q in range(vecs // 2):
            both = total[:, q * LANES : (q + 1) * LANES]
            lines += [(pair * both).sum(0, keepdims=True), (swapped * both).sum(0, keepdims=True)]
    lines = jnp.concatenate(lines, 0)
    shape = lines.shape
    row = lax.broadcasted_iota(jnp.int32, shape, 0)
    lane = lax.broadcasted_iota(jnp.int32, shape, 1)
    swap, q, p = row % 2, row // 2 % (vecs // 2), row // vecs
    first = 5 * vecs * vecs
    even = first + (2 * p + swap) * vecs + 2 * q
    odd = first + (2 * p + 1 - swap) * vecs + 2 * q + 1
    late = jnp.where(lane == even, lines[:, :BLOCK].sum(1, keepdims=True), 0.0)
    late += jnp.where(lane == odd, lines[:, BLOCK:].sum(1, keepdims=True), 0.0)
    late = late.sum(0, keepdims=True)
    packed = early_ref[...] + jnp.concatenate([late, jnp.zeros_like(late)], 0)
    gram_ref[...] = jnp.broadcast_to(packed[None], gram_ref.shape)


def totalled(vecs, parts, vectors, early, peers):
    whole = pl.BlockSpec(memory_space=pltpu.VMEM)
    return pl.pallas_call(
        functools.partial(total_kernel, vecs),
        out_shape=(
            jax.ShapeDtypeStruct(parts.shape[1:], F32),
            jax.ShapeDtypeStruct((peers, *early.shape), F32),
        ),
        in_specs=[whole] * 3,
        out_specs=(whole, whole),
        compiler_params=params(12),
        name="totalled",
    )(parts, vectors, early)


def unpack_kernel(vecs, scale, gram_ref, a_ref, b_ref):
    packed = gram_ref[0]
    for n in range(1, gram_ref.shape[0]):
        packed += gram_ref[n]
    packed = packed * scale
    lane = lax.broadcasted_iota(jnp.int32, (1, LANES), 1)
    late = 5 * vecs * vecs

    def assembled(runs):
        out = jnp.zeros((1, LANES), F32)
        for line, source, to, count in runs:
            by = (to - source) % LANES
            moved = packed[line : line + 1]
            moved = pltpu.roll(moved, by, 1) if by else moved
            out = jnp.where((lane >= to) & (lane < to + count), moved, out)
        return out[:, : 3 * vecs]

    def place(block, i, column):
        if block == 0:
            return 0, (5 * i + column) * vecs
        if block == 1:
            return 1, (4 * i + column - 1) * vecs
        return 1, (4 * vecs + 3 * i + column - 2) * vecs

    for m in range(3 * vecs):
        block, i = m // vecs, m % vecs
        runs = [(*place(block, i, column), column * vecs, vecs) for column in range(block, 3)]
        for column in range(block):
            for j in range(vecs):
                line, at = place(column, j, block)
                runs.append((line, at + i, column * vecs + j, 1))
        b_ref[m : m + 1, :] = assembled(runs)
        images = [(*place(block, i, 3), 0, vecs), (0, late + m * vecs, vecs, vecs)]
        a_ref[m : m + 1, :] = assembled(images + [(*place(block, i, 4), 2 * vecs, vecs)])


def unpacked(vecs, gram, scale):
    whole = pl.BlockSpec(memory_space=pltpu.VMEM)
    shape = jax.ShapeDtypeStruct((3 * vecs, 3 * vecs), F32)
    return pl.pallas_call(
        functools.partial(unpack_kernel, vecs, scale),
        out_shape=(shape, shape),
        in_specs=[whole],
        out_specs=(whole, whole),
        compiler_params=params(12),
        name="unpacked",
    )(gram)


def body(x_vec, hx_vec, p_vec, hp_vec, theta, precond, tile_vals, tile_rows, tile_cols, tile_count):
    vecs, piece_len = x_vec.shape
    rows, cols = lax.axis_size("row"), lax.axis_size("col")
    ring = rows // 2
    ndim_total = piece_len * rows * cols
    row_pos = lax.axis_index("row")
    width = piece_len // BLOCK
    slots = tile_vals.shape[2]
    tile = tile_vals[0, 0]
    residue = (hx_vec - x_vec * theta[:, None]) / precond[None, :]
    row_index = tile_rows[0, 0][None]
    col_index = tile_cols[0, 0][None]
    used = tile_count.reshape(1)

    def along(block, sign):
        path = [(r * cols + c, r * cols + (c + sign * r) % cols) for r in range(rows) for c in range(cols)]
        return lax.ppermute(block, BOTH, path)

    def within(block, flip, turn):
        return lax.ppermute(
            block, "row", [(i, (i // ring ^ flip) * ring + (i % ring + turn) % ring) for i in range(rows)]
        )

    own = residue.astype(BF16).reshape(vecs, width, BLOCK).transpose(0, 2, 1).reshape(vecs * BLOCK, width)
    across = within(own, 1, 0)
    pieces = [own, across] + [within(own, 0, n) for n in (1, 3, 2)]
    pieces += [within(across, 0, n) for n in (1, 3, 2)]
    order = jnp.arange(rows, dtype=jnp.int32)
    flips = sum(1 << n for n in (1, 5, 6, 7)) >> order & 1
    turns = sum(turn << 2 * n for n, turn in enumerate((0, 0, 1, 3, 2, 1, 3, 2))) >> 2 * order & 3
    bases = width * ((row_pos // ring ^ flips) * ring + (row_pos % ring + ring - turns) % ring)
    far_index = along(lax.optimization_barrier((row_index, pieces[2]))[0], 1)
    near = 5
    x_slots, held = early_pick(bases[:near], used, col_index, pieces[:near], tile)
    picked, far_order = pick(bases, far_index, pieces)
    far = along(picked, -1)
    forth, rest = forward(vecs, bases[near:], used, col_index, x_slots, pieces[near:], order_matrix(vecs), held, tile)
    forth = along(forth, 1)
    back = backward(vecs, far, route_matrix(vecs), held, rest)
    back = spread(used, col_index, back, rows * width, F32)
    every = jnp.full((1,), slots, jnp.int32)
    parts = spread(every, far_order, forth, rows * width, BF16, back).reshape(rows, width, vecs * BLOCK)
    vectors = jnp.concatenate([x_vec, residue, p_vec], 0)
    tied = lax.optimization_barrier((x_vec, residue, p_vec, hx_vec, hp_vec, parts))
    early = early_gram(vecs, *tied[:5])
    blocked = vectors.reshape(-1, width, BLOCK).transpose(1, 0, 2).reshape(width, -1)
    parts = lax.all_to_all(tied[5], "row", 0, 0, tiled=True)
    total, gram = totalled(vecs, parts, blocked, early, rows * cols)
    hw_vec = total.reshape(width, vecs, BLOCK).transpose(1, 0, 2).reshape(vecs, piece_len)
    gram = lax.all_to_all(gram, BOTH, 0, 0, tiled=True)
    gram_a, gram_b = unpacked(vecs, gram, 1.0 / ndim_total)
    return hw_vec, gram_a, gram_b


def solution(mesh):
    vector = P(None, ("col", "row"))
    placed = (
        vector,
        vector,
        vector,
        vector,
        P(),
        P(("col", "row")),
        P("row", "col", None, None),
        P("row", "col", None),
        P("row", "col", None),
        P("row", "col"),
    )
    return jax.shard_map(body, mesh=mesh, in_specs=placed, out_specs=(vector, P(), P()), check_vma=False)
```
